256 devices in a mesh: ep: 64 (over x, z, core), dp: 4 (over y).
Axes of the slice: x: 4, y: 4, z: 8, core: 2. Of those that a mesh axis runs over, the one named last changes fastest.
Arguments:
- tokens: bfloat16 [4096, 3584], P(('ep', 'dp')), may hold values from -6 to 6
- top_ids: int32 [4096, 8], P(('ep', 'dp')), may hold values from 0 to 127, all different within a row; in each aligned block of 16 rows (0 to 15, 16 to 31, ...) at most 2 rows name the same one
- gate_int: int32 [4096, 8], P(('ep', 'dp')), may hold values from 1 to 63
- replica_pick: int32 [4096, 8], P(('ep', 'dp')), may hold values 0 or 1
- plan: int32 [64], replicated, may hold values from 0 to 127, as said below
- gate_q: bfloat16 [128, 3584, 1024], P('ep', None, 'dp'), may hold values from -4 to 4
- gate_scale: bfloat16 [128, 28, 8], P('ep', None, 'dp'), may hold values from 0.008300781 to 0.033203125
- up_q: bfloat16 [128, 3584, 1024], P('ep', None, 'dp'), may hold values from -4 to 4
- up_scale: bfloat16 [128, 28, 8], P('ep', None, 'dp'), may hold values from 0.008300781 to 0.033203125
- down_q: bfloat16 [128, 1024, 3584], P('ep', 'dp'), may hold values from -4 to 4
- down_scale: bfloat16 [128, 8, 28], P('ep', 'dp'), may hold values from 0.015625 to 0.0625
Outputs:
- combined: bfloat16 [4096, 3584], P(('ep', 'dp'))
- slot_fill: float32 [64, 3, 256], P('ep')
- moved_down: bfloat16 [64, 1024, 3584], P('ep', 'dp')
- moved_down_scale: bfloat16 [64, 8, 28], P('ep', 'dp')
The draws below stay inside these ranges and needn't reach their ends.
Inputs may be any that keep to these rules, and one draw needn't show every extreme that they name: `top_ids`: no expert is named by more than 2 of the 16 rows of one device, and some expert reaches 2; the 8 experts of a row differ. `plan`: entry r is one of the 2 experts of ep index (r + m // 2) mod m, with m = 64.
All inputs are finite; a program needn't handle non-finite values. No bound on the sum of `replica_pick` on one device may be relied on, other than what follows from the above.
Results may differ from the reference program's by a relative error of at most 0.015.
Values may be sent and summed in bfloat16 or wider, within the bound.
A program may use at most 128 MiB of HBM per device.

```python
import math
import jax
import jax.numpy as jnp
import numpy as np
from jax import lax

D = 3584
FF = 1024
BLOCK = 128
TOPK = 8
EXP_DEV = 2
ROWS_DEV = 16
EXPERTS = 128
FF_DEV = 256
ROWS = 4096
MOST = 2
N_DP = 4
DEVICES = 256


def draw_plan(key, part):
    key = jax.random.fold_in(key, 7)
    n_groups = EXPERTS // EXP_DEV
    within = jax.random.randint(key, (n_groups,), 0, EXP_DEV)
    owner = (jnp.arange(n_groups, dtype=jnp.int32) + n_groups // 2) % n_groups
    return (owner * EXP_DEV + within).astype(jnp.int32)


def plant(values, own_key, low, largest):
    index_at = [jax.random.randint(jax.random.fold_in(own_key, axis), (), 0, length) for axis, length in enumerate(values.shape)]
    longest = values.shape.index(max(values.shape))
    neighbour = index_at[:longest] + [(index_at[longest] + 1) % values.shape[longest]] + index_at[longest + 1:]
    return values.at[tuple(index_at)].set(low).at[tuple(neighbour)].set(largest)


def steps_of(rng, extent, split, smallest, largest):
    def one(position, shards_of):
        heights = jax.random.uniform(jax.random.fold_in(jax.random.fold_in(rng, 6), position), (shards_of,), jnp.float32, smallest / len(split), largest / len(split))
        return jnp.repeat(jnp.exp(heights), extent[position] // shards_of).reshape((-1,) + (1,) * (len(extent) - position - 1))

    level = one(*split[0])
    for cut in split[1:]:
        level = level * one(*cut)
    return level


def assign_block(rng, own, number, rows, count, top, reach, skew):
    ranking = jax.random.permutation(rng, count)
    heavy_load, ordinary = shares(count, rows * top, reach, skew, True), shares(count, rows * top, reach, skew, False)
    places = jnp.arange(count)

    def named(sizes, turn):
        used = int((sizes > 0).sum())
        fixed = max(1, used // 4)
        moved = fixed + (places - fixed + turn * (used - fixed)) % max(1, count - fixed)
        return jnp.zeros((count,), jnp.int32).at[ranking[jnp.where(places < fixed, places, moved)]].set(jnp.asarray(sizes, jnp.int32))

    sizes = jnp.where(number % 4 == 0, named(heavy_load, number // 4), named(ordinary, number - number // 4 - 1))
    mixed = jax.random.permutation(jax.random.fold_in(own, 3), count)
    source_of, taker = mixed[0:count // 2 * 2:2], mixed[1:count // 2 * 2:2]
    slack = jnp.minimum(sizes[source_of] - 1, reach - sizes[taker]) // 2
    slack = jnp.where((source_of == ranking[0]) | (taker == ranking[0]) | (sizes[taker] == 0), 0, jnp.maximum(slack, 0))
    moved = jax.random.randint(jax.random.fold_in(own, 4), (count // 2,), 0, 1 << 20) % (slack + 1)
    sizes = sizes.at[source_of].add(-moved).at[taker].add(moved)
    members = jnp.searchsorted(jnp.cumsum(sizes), jnp.arange(rows * top), side="right").astype(jnp.int32)
    grid = members.reshape(top, rows).T
    grid = grid[jax.random.permutation(jax.random.fold_in(own, 1), rows)]
    turn = jax.random.randint(jax.random.fold_in(own, 2), (rows, 1), 0, top)
    return jnp.take_along_axis(grid, (jnp.arange(top)[None, :] + turn) % top, axis=1)


def shares(number_of, total, bound, lean, full):
    portions = [(1 << 20) // math.isqrt(rank ** lean) + 1 for rank in range(1, number_of + 1)]
    largest = bound if full else min(bound, max(-(-total // number_of), total * portions[0] // sum(portions)))
    least = 1 if total - largest >= number_of - 1 else 0
    given, spare = [largest] + [least] * (number_of - 1), total - largest - least * (number_of - 1)
    while spare > 0:
        candidates = [i for i in range(1, number_of) if given[i] < largest] or [i for i in range(1, number_of) if given[i] < bound]
        whole, budget = sum([portions[i] for i in candidates]), spare
        for i in candidates:
            extra = min(bound - given[i], max(1, budget * portions[i] // whole), spare)
            given[i] = given[i] + extra
            spare = spare - extra
    return np.array(given)


def noise(own_key, shape, width, limit, pieces=(), kind=jnp.bfloat16):
    values = width * jax.random.normal(own_key, shape, jnp.float32)
    if pieces:
        values = values * steps_of(own_key, shape, pieces, -0.22, 0.18)
    return jnp.clip(values, -limit, limit).astype(kind)


def setup_inputs(seed: int = 0) -> dict:
    arg_keys = jax.random.split(jax.random.key(seed), 12)
    tokens = noise(arg_keys[0], (ROWS, D), 1.0, 6.0, ((0, 256),))
    top_ids_keys = jax.random.split(jax.random.fold_in(arg_keys[1], 1), ROWS // ROWS_DEV)
    top_ids_turns = jax.random.permutation(jax.random.fold_in(arg_keys[1], 3), ROWS // ROWS_DEV)
    top_ids = jax.vmap(lambda own, number: assign_block(jax.random.fold_in(arg_keys[1], 2), own, number, ROWS_DEV, EXPERTS, TOPK, MOST, 2))(top_ids_keys, top_ids_turns).reshape((ROWS, TOPK))
    gate_int = plant(jax.random.randint(arg_keys[2], (ROWS, TOPK), 1, 64), jax.random.fold_in(arg_keys[2], 1), 1, 63).astype(jnp.int32)
    replica_pick = plant((jax.random.randint(arg_keys[3], (ROWS, TOPK), 0, 2) < 1).astype(jnp.int32), jax.random.fold_in(arg_keys[3], 1), 0, 1)
    plan = draw_plan(jax.random.fold_in(arg_keys[11], 71), 0)
    gate_q = noise(arg_keys[5], (EXPERTS, D, FF), 1.0, 4.0, ((0, 64), (2, 4)))
    gate_scale = jnp.clip(jnp.exp(math.log(0.033203125) - 1.3862944 * jax.random.uniform(arg_keys[6], (EXPERTS, D // BLOCK, FF // BLOCK), jnp.float32) ** steps_of(arg_keys[6], (EXPERTS, D // BLOCK, FF // BLOCK), ((0, 64), (2, 4)), -0.2, 0.2)), 0.008300781, 0.033203125).astype(jnp.bfloat16)
    up_q = noise(arg_keys[7], (EXPERTS, D, FF), 1.0, 4.0, ((0, 64), (2, 4)))
    up_scale = jnp.clip(jnp.exp(math.log(0.033203125) - 1.3862944 * jax.random.uniform(arg_keys[8], (EXPERTS, D // BLOCK, FF // BLOCK), jnp.float32) ** steps_of(arg_keys[8], (EXPERTS, D // BLOCK, FF // BLOCK), ((0, 64), (2, 4)), -0.2, 0.2)), 0.008300781, 0.033203125).astype(jnp.bfloat16)
    down_q = noise(arg_keys[9], (EXPERTS, FF, D), 1.0, 4.0, ((0, 64), (1, 4)))
    down_scale = jnp.clip(jnp.exp(math.log(0.0625) - 1.3862944 * jax.random.uniform(arg_keys[10], (EXPERTS, FF // BLOCK, D // BLOCK), jnp.float32) ** steps_of(arg_keys[10], (EXPERTS, FF // BLOCK, D // BLOCK), ((0, 64), (1, 4)), -0.2, 0.2)), 0.015625, 0.0625).astype(jnp.bfloat16)
    return {"tokens": tokens, "top_ids": top_ids, "gate_int": gate_int, "replica_pick": replica_pick, "plan": plan, "gate_q": gate_q, "gate_scale": gate_scale, "up_q": up_q, "up_scale": up_scale, "down_q": down_q, "down_scale": down_scale}


def dequant(quant, scales):
    rows_q, cols_q = quant.shape
    row_blocks, col_blocks = scales.shape
    blocked = quant.reshape(row_blocks, rows_q // row_blocks, col_blocks, cols_q // col_blocks).astype(jnp.float32)
    blocked = blocked * scales.astype(jnp.float32)[:, None, :, None]
    return blocked.reshape(rows_q, cols_q).astype(jnp.bfloat16)


def expert_apply(chosen, gate_w, up_w, down_w):
    summed = jnp.zeros((chosen.shape[0], down_w.shape[1]), jnp.float32)
    for quarter in range(N_DP):
        lower = quarter * FF_DEV
        gate_v = jnp.dot(chosen, gate_w[:, lower:lower + FF_DEV], preferred_element_type=jnp.float32)
        up_v = jnp.dot(chosen, up_w[:, lower:lower + FF_DEV], preferred_element_type=jnp.float32)
        hidden = (jax.nn.silu(gate_v) * up_v).astype(jnp.bfloat16)
        partial_value = jnp.dot(hidden, down_w[lower:lower + FF_DEV], preferred_element_type=jnp.float32).astype(jnp.bfloat16)
        partial_value = lax.optimization_barrier(partial_value)
        summed = summed + partial_value.astype(jnp.float32)
    return summed.astype(jnp.bfloat16)


def reference(tokens, top_ids, gate_int, replica_pick, plan, gate_q, gate_scale, up_q, up_scale, down_q, down_scale):
    flat_ids = top_ids.reshape(-1).astype(jnp.int32)
    total_assign = flat_ids.shape[0]
    gate_frac = gate_int.astype(jnp.float32)
    gate_frac = gate_frac / jnp.sum(gate_frac, axis=-1, keepdims=True)
    flat_frac = gate_frac.reshape(-1)
    sorted_at = jnp.argsort(flat_ids, stable=True).astype(jnp.int32)
    counts = jax.ops.segment_sum(jnp.ones_like(flat_ids), flat_ids, num_segments=EXPERTS).astype(jnp.int32)
    starts = (jnp.cumsum(counts) - counts).astype(jnp.int32)
    capacity = DEVICES * MOST

    def expert_step(running, expert_id):
        offsets = jnp.arange(capacity, dtype=jnp.int32)
        is_live = offsets < counts[expert_id]
        assign = sorted_at[jnp.clip(starts[expert_id] + offsets, 0, total_assign - 1)]
        row_ids = (assign // TOPK).astype(jnp.int32)
        chosen = tokens[row_ids]
        gate_w = dequant(gate_q[expert_id], gate_scale[expert_id])
        up_w = dequant(up_q[expert_id], up_scale[expert_id])
        down_w = dequant(down_q[expert_id], down_scale[expert_id])
        result = expert_apply(chosen, gate_w, up_w, down_w)
        scaled = jnp.where(is_live, flat_frac[assign], jnp.float32(0.0))
        running = running.at[row_ids].add(scaled[:, None] * result.astype(jnp.float32))
        return running, None

    running = jnp.zeros((tokens.shape[0], tokens.shape[1]), jnp.float32)
    running, _ = lax.scan(expert_step, running, jnp.arange(EXPERTS, dtype=jnp.int32))
    combined = running.astype(jnp.bfloat16)

    n_groups = EXPERTS // EXP_DEV
    home_ep = flat_ids // EXP_DEV
    partner = (home_ep + n_groups // 2) % n_groups
    to_copy = (plan[partner] == flat_ids) & (replica_pick.reshape(-1) == 1)
    target = jnp.where(to_copy, partner, home_ep)
    slot_idx = jnp.where(to_copy, EXP_DEV, flat_ids % EXP_DEV)
    source = (jnp.arange(total_assign, dtype=jnp.int32) // TOPK) // ROWS_DEV
    bucket = ((target * (EXP_DEV + 1) + slot_idx) * DEVICES + source).astype(jnp.int32)
    tallies = jax.ops.segment_sum(jnp.ones((total_assign,), jnp.float32), bucket, num_segments=n_groups * (EXP_DEV + 1) * DEVICES)
    slot_fill = tallies.reshape(n_groups, EXP_DEV + 1, DEVICES) / jnp.float32(MOST)
    plan_ids = plan.astype(jnp.int32)
    moved_down = down_q[plan_ids]
    moved_down_scale = down_scale[plan_ids]
    return combined, slot_fill, moved_down, moved_down_scale
```

```python
import functools

import jax
import jax.numpy as jnp
from jax import lax
from jax.experimental import pallas as pl
from jax.experimental.pallas import tpu as pltpu
from jax.sharding import PartitionSpec as P

NX, NZ, NC, NY = 4, 8, 2, 4
N_EP = NX * NZ * NC
ROWS = 16
TOPK = 8
EXP_DEV = 2
MOST = 2
CAP = N_EP * MOST
SLOTS = EXP_DEV * CAP
PLANE = N_EP * ROWS
D = 3584
FF = 256
BLOCK = 128
CW = 512
NCH = D // CW
RB = CW // BLOCK
F32 = jnp.float32
BF16 = jnp.bfloat16
MESH = pl.DeviceIdType.MESH


def kernel(
    tok, meta, gs, us, ds, gq_hbm, uq_hbm, dq_hbm,
    comb, cnt,
    dense, mg, xs, gq, uq, dq, accg, accu, hid, ryh, ryf, crecv, zrecv, xrecv,
    pack, unpack, wslot, cntbuf,
    w_sem, xi_s, xi_r, zi_s, zi_r, ci_s, ci_r, yi_s, yi_r, m_s, m_r,
    yo_s, yo_r, co_s, co_r, zo_s, zo_r, xo_s, xo_r, n_s, n_r,
):
    ep = lax.axis_index("ep")
    y = lax.axis_index("dp")
    c = ep % NC
    z = (ep // NC) % NZ
    x = ep // (NC * NZ)
    way = 1 - 2 * c
    y_up, y_dn, y_op = (y + 1) % NY, (y + NY - 1) % NY, (y + 2) % NY

    def zat(k):
        return (z + way * k + 2 * NZ) % NZ

    def xat(k):
        return (x + way * k + 2 * NX) % NX

    def at_x(k):
        return {"ep": (xat(k) * NZ + z) * NC + c, "dp": y}

    def at_z(k):
        return {"ep": (x * NZ + zat(k)) * NC + c, "dp": y}

    def at_y(to):
        return {"ep": ep, "dp": to}

    other = {"ep": (x * NZ + z) * NC + 1 - c, "dp": y}

    def remote(src, dst, ssem, rsem, dev):
        return pltpu.make_async_remote_copy(
            src_ref=src, dst_ref=dst, send_sem=ssem, recv_sem=rsem,
            device_id=dev, device_id_type=MESH,
        )

    def xblock(ref, core, zz, xx):
        return ref.at[pl.ds(core * NZ * NX + zz * NX + xx, 1)]

    def zblock(ref, core, zz):
        return ref.at[pl.ds(core * NZ * NX + zz * NX, NX)]

    def cblock(ref, core):
        return ref.at[pl.ds(core * NZ * NX, NZ * NX)]

    def g_x(ref, ss, rs, k, sent):
        off, hop = ((0, 1), (-1, 1), (0, -1))[k]
        if not sent:
            off = off - hop
        b = xblock(ref, c, z, xat(off))
        return remote(b, b, ss, rs, at_x(hop))

    def g_z(ref, ss, rs, k, sent):
        off, hop = ((0, 1), (-1, 1), (-2, 1), (-3, 1), (0, -1), (1, -1), (2, -1))[k]
        if not sent:
            off = off - hop
        b = zblock(ref, c, zat(off))
        return remote(b, b, ss, rs, at_z(hop))

    def g_c(ref, ss, rs, off):
        b = zblock(ref, c, zat(off))
        return remote(b, b, ss, rs, other)

    def g_c_all(ref, ss, rs, core):
        b = cblock(ref, core)
        return remote(b, b, ss, rs, other)

    def both(j, fn):
        fn(dense.at[j], (xi_s.at[j], xi_r.at[j], zi_s.at[j], zi_r.at[j], ci_s.at[j], ci_r.at[j]))

        @pl.when(j == 0)
        def _():
            fn(mg, (m_s.at[pl.ds(0, 3)], m_r.at[pl.ds(0, 3)], m_s.at[pl.ds(3, 7)],
                    m_r.at[pl.ds(3, 7)], m_s.at[10], m_r.at[10]))

    def x_start(j, k):
        both(j, lambda ref, q: g_x(ref, q[0].at[k], q[1].at[k], k, True).start())

    def x_recv(j, k):
        both(j, lambda ref, q: g_x(ref, q[0].at[k], q[1].at[k], k, False).wait_recv())

    def x_sent(j, k):
        both(j, lambda ref, q: g_x(ref, q[0].at[k], q[1].at[k], k, True).wait_send())

    def z_start(j, k):
        both(j, lambda ref, q: g_z(ref, q[2].at[k], q[3].at[k], k, True).start())

    def z_recv(j, k):
        both(j, lambda ref, q: g_z(ref, q[2].at[k], q[3].at[k], k, False).wait_recv())

    def z_sent(j, k):
        both(j, lambda ref, q: g_z(ref, q[2].at[k], q[3].at[k], k, True).wait_send())

    def c_start(j, off):
        both(j, lambda ref, q: g_c(ref, q[4], q[5], off).start())

    def c_recv(j):
        both(j, lambda ref, q: g_c_all(ref, q[4], q[5], 1 - c).wait_recv())

    def c_sent(j):
        both(j, lambda ref, q: g_c_all(ref, q[4], q[5], c).wait_send())

    half = SLOTS // 2

    def g_y(j, k, sent):
        if k < 2:
            to = (y_up, y_dn)[k]
            b = xs.at[j, y if sent else (y_dn, y_up)[k]]
        else:
            to = (y_up, y_dn)[k - 2]
            plane = (y_dn, y_up)[k - 2] if sent else y_op
            b = xs.at[j, plane, pl.ds((k - 2) * half, half)]
        return remote(b, b, yi_s.at[j, k], yi_r.at[j, k], at_y(to))

    barrier = pltpu.get_barrier_semaphore()
    partners = (at_x(1), at_x(-1), at_z(1), at_z(-1), other, at_y(y_up), at_y(y_dn), at_y(y_op))
    for dev in partners:
        pl.semaphore_signal(barrier, inc=1, device_id=dev, device_id_type=MESH)

    loads = [
        pltpu.make_async_copy(a, b, w_sem.at[i])
        for i, (a, b) in enumerate(((gq_hbm, gq), (uq_hbm, uq), (dq_hbm, dq)))
    ]
    for load in loads:
        load.start()
    own = c * NZ * NX + z * NX + x
    mg[own] = meta[...]
    for j in range(NCH):
        dense[j, own] = tok[:, j * CW:(j + 1) * CW]
    accg[...] = jnp.zeros_like(accg)
    accu[...] = jnp.zeros_like(accu)
    pl.semaphore_wait(barrier, len(partners))

    def x_begin(j, carry):
        x_start(j, 0)
        x_start(j, 2)
        return carry

    lax.fori_loop(0, NCH, x_begin, 0)

    def n_copy(k, sent):
        to = (y_up, y_dn, y_op)[k]
        b = cntbuf.at[y if sent else (y_dn, y_up, y_op)[k]]
        return remote(b, b, n_s.at[k], n_r.at[k], at_y(to))

    def routes():
        def rows_of(i):
            return mg[pl.ds(i * 8, 8)].reshape(BLOCK, BLOCK).astype(F32)

        lane = lax.broadcasted_iota(jnp.int32, (BLOCK, BLOCK), 1)
        row = lax.broadcasted_iota(jnp.int32, (BLOCK, BLOCK), 0)
        before = (lane < row).astype(BF16)
        first = (ep * EXP_DEV).astype(F32)
        slot0 = (ep * (EXP_DEV + 1)).astype(F32)
        fills = jnp.zeros((BLOCK, N_EP * NY), F32)
        sofar = jnp.zeros((1, BLOCK), F32)
        wsum = jnp.zeros((SLOTS, 1), F32)
        for i in range(PLANE // BLOCK):
            m = rows_of(i)
            gates = pltpu.roll(m, BLOCK - TOPK, 1)
            is_id = lane < TOPK
            den = jnp.sum(jnp.where(is_id, gates, 0.0), axis=1, keepdims=True)
            flags, weights = [], []
            for e in range(EXP_DEV):
                hit = is_id & (m == first + e)
                flags.append(jnp.sum(jnp.where(hit, 1.0, 0.0), axis=1, keepdims=True))
                weights.append(jnp.sum(jnp.where(hit, gates, 0.0), axis=1, keepdims=True) / den)
            flag = jnp.where(lane == 0, flags[0], jnp.where(lane == 1, flags[1], 0.0))
            place = jnp.dot(before, flag.astype(BF16), preferred_element_type=F32) + sofar
            sofar = sofar + jnp.sum(flag, axis=0, keepdims=True)
            spread = []
            for e in range(EXP_DEV):
                at = jnp.sum(jnp.where(lane == e, place, 0.0), axis=1, keepdims=True)
                at = at.astype(jnp.int32)
                spread.append(jnp.where((lane == at) & (flags[e] > 0.0), weights[e], 0.0))
            spread = jnp.concatenate(spread, axis=1)
            chosen = jnp.where(spread > 0.0, 1.0, 0.0)
            unpack[i * BLOCK:(i + 1) * BLOCK, :] = chosen.astype(BF16)
            turned = jnp.transpose(spread)
            pack[:, i * BLOCK:(i + 1) * BLOCK] = jnp.where(turned > 0.0, 1.0, 0.0).astype(BF16)
            wsum = wsum + jnp.sum(turned, axis=1, keepdims=True)
            keyed = (lane >= 2 * TOPK) & (lane < 3 * TOPK)
            tally = jnp.zeros((BLOCK, BLOCK), F32)
            for s in range(EXP_DEV + 1):
                n = jnp.sum(jnp.where(keyed & (m == slot0 + s), 1.0, 0.0), axis=1, keepdims=True)
                tally = tally + jnp.where(lane == s, n, 0.0)
            r = lax.broadcasted_iota(jnp.int32, (BLOCK, N_EP * NY), 0) + i * BLOCK
            col = lax.broadcasted_iota(jnp.int32, (BLOCK, N_EP * NY), 1)
            b = r >> 4
            source = (b & 3) * (NZ * NC) + ((b >> 2) & 7) * NC + (b >> 5)
            mine = (col == source * NY + y).astype(BF16)
            fills = fills + jnp.dot(jnp.transpose(tally).astype(BF16), mine, preferred_element_type=F32)
        wslot[...] = jnp.broadcast_to(wsum, (SLOTS, BLOCK))
        cntbuf[y] = fills[0:8]
        for k in range(3):
            n_copy(k, True).start()

    def weight(q, e, j, s):
        parts = []
        for i in range(RB):
            at = (j * RB + i) * 2
            row = jnp.where(
                lax.broadcasted_iota(jnp.int32, (1, FF), 1) < BLOCK, s[e, at], s[e, at + 1]
            )
            rows = q[e, pl.ds(pl.multiple_of(j * CW + i * BLOCK, BLOCK), BLOCK), :]
            parts.append((rows.astype(F32) * row).astype(BF16))
        return jnp.concatenate(parts, axis=0)

    def stage(t, late, fn):
        j = t - late

        @pl.when((j >= 0) & (j < NCH))
        def _():
            fn(j)

    def i1(j):
        x_recv(j, 0)
        x_start(j, 1)

    def i2(j):
        x_recv(j, 2)
        x_recv(j, 1)
        z_start(j, 0)
        z_start(j, 4)
        c_start(j, 0)

    def i3(j):
        z_recv(j, 0)
        z_start(j, 1)
        z_recv(j, 4)
        z_start(j, 5)
        c_start(j, -1)
        c_start(j, 1)

    def i4(j):
        z_recv(j, 1)
        z_start(j, 2)
        z_recv(j, 5)
        z_start(j, 6)
        c_start(j, -2)
        c_start(j, 2)

    def i5(j):
        z_recv(j, 2)
        z_start(j, 3)
        c_start(j, -3)
        z_recv(j, 6)
        c_start(j, 3)

    def i6(j):
        z_recv(j, 3)
        c_start(j, -4)

    def i7(j):
        c_recv(j)

        @pl.when(j == 0)
        def _():
            routes()

        full = dense[j].reshape(PLANE, CW)
        xs[j, y] = jnp.dot(pack[...], full, preferred_element_type=F32).astype(BF16)
        g_y(j, 0, True).start()
        g_y(j, 1, True).start()

    def i8(j):
        g_y(j, 0, False).wait_recv()
        g_y(j, 2, True).start()
        g_y(j, 1, False).wait_recv()
        g_y(j, 3, True).start()

    def i9(j):
        @pl.when(j == 0)
        def _():
            loads[0].wait()
            loads[1].wait()

        g_y(j, 2, False).wait_recv()
        g_y(j, 3, False).wait_recv()
        for e in range(EXP_DEV):
            rows = xs[j, :, e * CAP:(e + 1) * CAP, :].reshape(NY * CAP, CW)
            accg[e] += jnp.dot(rows, weight(gq, e, j, gs), preferred_element_type=F32)
            accu[e] += jnp.dot(rows, weight(uq, e, j, us), preferred_element_type=F32)

    def in_tick(t, carry):
        for late, fn in enumerate((i1, i2, i3, i4, i5, i6, i7, i8, i9)):
            stage(t, late, fn)
        return carry

    lax.fori_loop(0, NCH + 8, in_tick, 0)

    for e in range(EXP_DEV):
        v = accg[e]
        hid[e] = (v / (1.0 + jnp.exp(-v)) * accu[e]).astype(BF16)

    def in_done(j, carry):
        for k in range(3):
            x_sent(j, k)
        for k in range(7):
            z_sent(j, k)
        c_sent(j)
        for k in range(4):
            g_y(j, k, True).wait_send()
        return carry

    lax.fori_loop(0, NCH, in_done, 0)
    for k in range(3):
        n_copy(k, False).wait_recv()
    cnt[...] = (cntbuf[0] + cntbuf[1] + cntbuf[2] + cntbuf[3]) * (1.0 / MOST)
    loads[2].wait()

    def o_y(j, k, sent):
        to = (y_up, y_dn)[k % 2]
        if k < 2:
            src = xs.at[j, y_op, pl.ds(k * half, half)]
            dst = ryh.at[j, k]
        else:
            src = xs.at[j, to]
            dst = ryf.at[j, k - 2]
        return remote(src, dst, yo_s.at[j, k], yo_r.at[j, k], at_y(to))

    def o_c(j):
        return remote(cblock(dense.at[j], 1 - c), crecv.at[j], co_s.at[j], co_r.at[j], other)

    z_steps = ((4, 1), (3, 1), (2, 1), (1, 1), (-3, -1), (-2, -1), (-1, -1))

    def o_z(j, k):
        off, hop = z_steps[k]
        return remote(zblock(dense.at[j], c, zat(off)), zrecv.at[j, k],
                      zo_s.at[j, k], zo_r.at[j, k], at_z(hop))

    x_steps = ((2, 1), (1, 1), (-1, -1))

    def o_x(j, k):
        off, hop = x_steps[k]
        return remote(xblock(dense.at[j], c, z, xat(off)), xrecv.at[j, pl.ds(k, 1)],
                      xo_s.at[j, k], xo_r.at[j, k], at_x(hop))

    def add(a, b):
        return (a.astype(F32) + b.astype(F32)).astype(BF16)

    def add_z(j, k):
        off, hop = z_steps[k]
        o_z(j, k).wait_recv()
        at = pl.ds(c * NZ * NX + zat(off - hop) * NX, NX)
        dense[j, at] = add(dense[j, at], zrecv[j, k])

    def o0(j):
        cols = pl.ds(pl.multiple_of(j * CW, CW), CW)
        for e in range(EXP_DEV):
            parts = []
            for r in range(FF // BLOCK):
                row = jnp.concatenate(
                    [jnp.full((1, BLOCK), ds[e, r * (D // BLOCK) + j * RB + i], F32) for i in range(RB)],
                    axis=1,
                )
                rows = dq[e, r * BLOCK:(r + 1) * BLOCK, cols]
                parts.append((rows.astype(F32) * row).astype(BF16))
            w = jnp.concatenate(parts, axis=0)
            out = jnp.dot(hid[e], w, preferred_element_type=F32).astype(BF16)
            xs[j, :, e * CAP:(e + 1) * CAP, :] = out.reshape(NY, CAP, CW)
        o_y(j, 0, True).start()
        o_y(j, 1, True).start()

    def o1(j):
        for k in range(2):
            o_y(j, k, False).wait_recv()
            to = (y_up, y_dn)[k]
            at = pl.ds(k * half, half)
            xs[j, to, at] = add(xs[j, to, at], ryh[j, k])
            o_y(j, 2 + k, True).start()

    def o2(j):
        o_y(j, 2, False).wait_recv()
        o_y(j, 3, False).wait_recv()
        total = xs[j, y].astype(F32) + ryf[j, 0].astype(F32) + ryf[j, 1].astype(F32)
        scaled = (total * wslot[:, 0:1]).astype(BF16)
        n = 256
        for i in range(PLANE // n):
            out = jnp.dot(unpack[i * n:(i + 1) * n, :], scaled, preferred_element_type=F32)
            dense[j, i * (n // ROWS):(i + 1) * (n // ROWS)] = out.astype(BF16).reshape(n // ROWS, ROWS, CW)
        o_c(j).start()

    def o3(j):
        o_c(j).wait_recv()
        at = pl.ds(c * NZ * NX, NZ * NX)
        dense[j, at] = add(dense[j, at], crecv[j])
        o_z(j, 0).start()
        o_z(j, 4).start()

    def o4(j):
        add_z(j, 0)
        o_z(j, 1).start()
        add_z(j, 4)
        o_z(j, 5).start()

    def o5(j):
        add_z(j, 1)
        o_z(j, 2).start()
        add_z(j, 5)
        o_z(j, 6).start()

    def o6(j):
        add_z(j, 2)
        o_z(j, 3).start()

    def o7(j):
        add_z(j, 3)
        add_z(j, 6)
        o_x(j, 0).start()
        o_x(j, 2).start()

    def o8(j):
        o_x(j, 0).wait_recv()
        at = c * NZ * NX + z * NX + xat(1)
        dense[j, at] = add(dense[j, at], xrecv[j, 0])
        o_x(j, 1).start()

    def o9(j):
        o_x(j, 1).wait_recv()
        o_x(j, 2).wait_recv()
        total = dense[j, own].astype(F32) + xrecv[j, 1].astype(F32) + xrecv[j, 2].astype(F32)
        comb[:, pl.ds(pl.multiple_of(j * CW, CW), CW)] = total.astype(BF16)

    def out_tick(t, carry):
        for late, fn in enumerate((o0, o1, o2, o3, o4, o5, o6, o7, o8, o9)):
            stage(t, late, fn)
        return carry

    lax.fori_loop(0, NCH + 9, out_tick, 0)

    def out_done(j, carry):
        for k in range(4):
            o_y(j, k, True).wait_send()
        o_c(j).wait_send()
        for k in range(7):
            o_z(j, k).wait_send()
        for k in range(3):
            o_x(j, k).wait_send()
        return carry

    lax.fori_loop(0, NCH, out_done, 0)
    for k in range(3):
        n_copy(k, True).wait_send()


def layer(tok, meta, gs, us, ds, gq, uq, dq):
    vmem = pl.BlockSpec(memory_space=pltpu.VMEM)
    smem = pl.BlockSpec(memory_space=pltpu.SMEM)
    hbm = pl.BlockSpec(memory_space=pl.ANY)
    dma = pltpu.SemaphoreType.DMA
    blocks = NC * NZ * NX
    return pl.pallas_call(
        kernel,
        out_shape=(
            jax.ShapeDtypeStruct((ROWS, D), BF16),
            jax.ShapeDtypeStruct((8, N_EP * NY), F32),
        ),
        in_specs=[vmem, vmem, smem, smem, smem, hbm, hbm, hbm],
        out_specs=(vmem, vmem),
        scratch_shapes=[
            pltpu.VMEM((NCH, blocks, ROWS, CW), BF16),
            pltpu.VMEM((blocks, ROWS, BLOCK), BF16),
            pltpu.VMEM((NCH, NY, SLOTS, CW), BF16),
            pltpu.VMEM((EXP_DEV, D, FF), BF16),
            pltpu.VMEM((EXP_DEV, D, FF), BF16),
            pltpu.VMEM((EXP_DEV, FF, D), BF16),
            pltpu.VMEM((EXP_DEV, NY * CAP, FF), F32),
            pltpu.VMEM((EXP_DEV, NY * CAP, FF), F32),
            pltpu.VMEM((EXP_DEV, NY * CAP, FF), BF16),
            pltpu.VMEM((NCH, 2, SLOTS // 2, CW), BF16),
            pltpu.VMEM((NCH, 2, SLOTS, CW), BF16),
            pltpu.VMEM((NCH, blocks // 2, ROWS, CW), BF16),
            pltpu.VMEM((NCH, 7, NX, ROWS, CW), BF16),
            pltpu.VMEM((NCH, 3, ROWS, CW), BF16),
            pltpu.VMEM((SLOTS, PLANE), BF16),
            pltpu.VMEM((PLANE, SLOTS), BF16),
            pltpu.VMEM((SLOTS, BLOCK), F32),
            pltpu.VMEM((NY, 8, N_EP * NY), F32),
            dma((3,)),
            dma((NCH, 3)), dma((NCH, 3)),
            dma((NCH, 7)), dma((NCH, 7)),
            dma((NCH,)), dma((NCH,)),
            dma((NCH, 4)), dma((NCH, 4)),
            dma((11,)), dma((11,)),
            dma((NCH, 4)), dma((NCH, 4)),
            dma((NCH,)), dma((NCH,)),
            dma((NCH, 7)), dma((NCH, 7)),
            dma((NCH, 3)), dma((NCH, 3)),
            dma((3,)), dma((3,)),
        ],
        compiler_params=pltpu.CompilerParams(
            collective_id=0, has_side_effects=True, vmem_limit_bytes=60 * 1024 * 1024
        ),
        cost_estimate=pl.CostEstimate(
            flops=6_000_000_000, bytes_accessed=400_000_000, transcendentals=0
        ),
    )(tok, meta, gs, us, ds, gq, uq, dq)


def slot_keys(top_ids, replica_pick, plan):
    home = top_ids // EXP_DEV
    partner = (home + N_EP // 2) % N_EP
    held = jnp.sum(
        jnp.where(partner[..., None] == jnp.arange(N_EP, dtype=jnp.int32), plan, 0), axis=-1
    )
    moved = (held == top_ids) & (replica_pick == 1)
    target = jnp.where(moved, partner, home)
    return target * (EXP_DEV + 1) + jnp.where(moved, EXP_DEV, top_ids % EXP_DEV)


def per_device(
    tokens, top_ids, gate_int, replica_pick, plan,
    gate_q, gate_scale, up_q, up_scale, down_q, down_scale,
):
    ep = lax.axis_index("ep")
    receiver = (ep + N_EP // 2) % N_EP
    wanted = plan[receiver] - ep * EXP_DEV
    route = [((i + N_EP // 2) % N_EP, i) for i in range(N_EP)]
    moved_down, moved_scale = (
        lax.ppermute(lax.dynamic_index_in_dim(a, wanted, 0, keepdims=True), "ep", route)
        for a in (down_q, down_scale)
    )
    keys = slot_keys(top_ids, replica_pick, plan)
    meta = jnp.concatenate([top_ids, gate_int, keys], axis=1).astype(BF16)
    meta = jnp.pad(meta, ((0, 0), (0, BLOCK - 3 * TOPK)))
    combined, fill = layer(
        tokens, meta,
        gate_scale.astype(F32).reshape(EXP_DEV, -1),
        up_scale.astype(F32).reshape(EXP_DEV, -1),
        down_scale.astype(F32).reshape(EXP_DEV, -1),
        gate_q, up_q, down_q,
    )
    return combined, fill[None, :EXP_DEV + 1], moved_down, moved_scale


def solution(mesh):
    return jax.shard_map(
        per_device,
        mesh=mesh,
        in_specs=(
            P(("ep", "dp"), None),
            P(("ep", "dp"), None),
            P(("ep", "dp"), None),
            P(("ep", "dp"), None),
            P(),
            P("ep", None, "dp"),
            P("ep", None, "dp"),
            P("ep", None, "dp"),
            P("ep", None, "dp"),
            P("ep", "dp", None),
            P("ep", "dp", None),
        ),
        out_specs=(
            P(("ep", "dp"), None),
            P("ep", None, None),
            P("ep", "dp", None),
            P("ep", "dp", None),
        ),
        check_vma=False,
    )
```

```python
import functools

import jax
import jax.numpy as jnp
from jax import lax
from jax.experimental import pallas as pl
from jax.experimental.pallas import tpu as pltpu
from jax.sharding import PartitionSpec as P

NX, NZ, NC, NY = 4, 8, 2, 4
N_EP = NX * NZ * NC
ROWS = 16
TOPK = 8
EXP_DEV = 2
MOST = 2
CAP = N_EP * MOST
SLOTS = EXP_DEV * CAP
PLANE = N_EP * ROWS
D = 3584
FF = 256
BLOCK = 128
CW = 256
NCH = D // CW
RB = CW // BLOCK
F32 = jnp.float32
BF16 = jnp.bfloat16
MESH = pl.DeviceIdType.MESH


def kernel(
    tok, ids_t, gates_t, picks_t, plan, gs, us, ds, gq_hbm, uq_hbm, dq_hbm,
    comb, cnt, moved, moved_s,
    dense, mg, xs, gq, uq, dq, accg, accu, hid, ryh, ryf, crecv, zrecv, xrecv,
    pack, unpack, wslot, cntbuf, sel, sel_s, got_s, grow, urow, drow,
    w_sem, mv_s, mv_r, xi_s, xi_r, zi_s, zi_r, ci_s, ci_r, yi_s, yi_r, m_s, m_r,
    yo_s, yo_r, co_s, co_r, zo_s, zo_r, xo_s, xo_r, n_s, n_r,
):
    ep = lax.axis_index("ep")
    y = lax.axis_index("dp")
    c = ep % NC
    z = (ep // NC) % NZ
    x = ep // (NC * NZ)
    way = 1 - 2 * c
    y_up, y_dn, y_op = (y + 1) % NY, (y + NY - 1) % NY, (y + 2) % NY

    def zat(k):
        return (z + way * k + 2 * NZ) % NZ

    def xat(k):
        return (x + way * k + 2 * NX) % NX

    def at_x(k):
        return {"ep": (xat(k) * NZ + z) * NC + c, "dp": y}

    def at_z(k):
        return {"ep": (x * NZ + zat(k)) * NC + c, "dp": y}

    def at_y(to):
        return {"ep": ep, "dp": to}

    other = {"ep": (x * NZ + z) * NC + 1 - c, "dp": y}

    def remote(src, dst, ssem, rsem, dev):
        return pltpu.make_async_remote_copy(
            src_ref=src, dst_ref=dst, send_sem=ssem, recv_sem=rsem,
            device_id=dev, device_id_type=MESH,
        )

    def xblock(ref, core, zz, xx):
        return ref.at[pl.ds(core * NZ * NX + zz * NX + xx, 1)]

    def zblock(ref, core, zz):
        return ref.at[pl.ds(core * NZ * NX + zz * NX, NX)]

    def cblock(ref, core):
        return ref.at[pl.ds(core * NZ * NX, NZ * NX)]

    def g_x(ref, ss, rs, k, sent):
        hop = (1, -1, 2)[k]
        b = xblock(ref, c, z, xat(0 if sent else -hop))
        return remote(b, b, ss, rs, at_x(hop))

    def g_z(ref, ss, rs, k, sent):
        off, hop = ((0, 1), (0, -1), (0, 2), (0, -2), (-2, 1), (2, -1), (-2, 2))[k]
        if not sent:
            off = off - hop
        b = zblock(ref, c, zat(off))
        return remote(b, b, ss, rs, at_z(hop))

    def g_c(ref, ss, rs, core):
        b = cblock(ref, core)
        return remote(b, b, ss, rs, other)

    def both(j, fn):
        @pl.when(j == 0)
        def _():
            fn(mg, (m_s.at[pl.ds(0, 3)], m_r.at[pl.ds(0, 3)], m_s.at[pl.ds(3, 7)],
                    m_r.at[pl.ds(3, 7)], m_s.at[10], m_r.at[10]))

        fn(dense.at[j], (xi_s.at[j], xi_r.at[j], zi_s.at[j], zi_r.at[j], ci_s.at[j], ci_r.at[j]))

    def x_start(j, k):
        both(j, lambda ref, q: g_x(ref, q[0].at[k], q[1].at[k], k, True).start())

    def x_recv(j, k):
        both(j, lambda ref, q: g_x(ref, q[0].at[k], q[1].at[k], k, False).wait_recv())

    def x_sent(j, k):
        both(j, lambda ref, q: g_x(ref, q[0].at[k], q[1].at[k], k, True).wait_send())

    def z_start(j, k):
        both(j, lambda ref, q: g_z(ref, q[2].at[k], q[3].at[k], k, True).start())

    def z_recv(j, k):
        both(j, lambda ref, q: g_z(ref, q[2].at[k], q[3].at[k], k, False).wait_recv())

    def z_sent(j, k):
        both(j, lambda ref, q: g_z(ref, q[2].at[k], q[3].at[k], k, True).wait_send())

    def c_start(j):
        both(j, lambda ref, q: g_c(ref, q[4], q[5], c).start())

    def c_recv(j):
        both(j, lambda ref, q: g_c(ref, q[4], q[5], 1 - c).wait_recv())

    def c_sent(j):
        both(j, lambda ref, q: g_c(ref, q[4], q[5], c).wait_send())

    half = SLOTS // 2

    def g_y(j, k, sent):
        if k < 2:
            to = (y_up, y_dn)[k]
            b = xs.at[j, y if sent else (y_dn, y_up)[k]]
        else:
            to = (y_up, y_dn)[k - 2]
            plane = (y_dn, y_up)[k - 2] if sent else y_op
            b = xs.at[j, plane, pl.ds((k - 2) * half, half)]
        return remote(b, b, yi_s.at[j, k], yi_r.at[j, k], at_y(to))

    def routing_values():
        ids = ids_t[...]
        planned = ids == plan[0]
        for r in range(1, N_EP):
            planned = planned | (ids == plan[r])
        there = planned & (picks_t[...] == 1)
        home = ids >> 1
        target = jnp.where(there, (home + N_EP // 2) & (N_EP - 1), home)
        key = target * (EXP_DEV + 1) + jnp.where(there, EXP_DEV, ids & 1)
        cols = jnp.concatenate([ids, gates_t[...], key], axis=0).astype(F32).astype(BF16)
        n = 3 * TOPK
        place = lax.broadcasted_iota(jnp.int32, (n, BLOCK), 0) == lax.broadcasted_iota(jnp.int32, (n, BLOCK), 1)
        return lax.dot_general(
            cols, place.astype(BF16), (((0,), (0,)), ((), ())), preferred_element_type=F32
        ).astype(BF16)

    def spread_scales():
        side = lax.broadcasted_iota(jnp.int32, (2, FF), 0) == lax.broadcasted_iota(jnp.int32, (2, FF), 1) // BLOCK
        n = D // BLOCK
        wide = lax.broadcasted_iota(jnp.int32, (n, D), 0) == lax.broadcasted_iota(jnp.int32, (n, D), 1) // BLOCK
        for e in range(EXP_DEV):
            for src, dst in ((gs, grow), (us, urow)):
                dst[e] = lax.dot_general(
                    src[e], side.astype(BF16), (((0,), (0,)), ((), ())), preferred_element_type=F32
                )
            drow[e] = jnp.dot(ds[e], wide.astype(BF16), preferred_element_type=F32)

    def mv(j):
        cols = slice(None) if j is None else pl.ds(pl.multiple_of(j * CW, CW), CW)
        return remote(sel.at[:, cols], moved.at[0, :, cols], mv_s.at[0], mv_r.at[0], at_x(2))

    def mv_scale():
        return remote(sel_s, got_s, mv_s.at[1], mv_r.at[1], at_x(2))

    def select_moved():
        loads[2].wait()
        wanted = plan[(ep + N_EP // 2) % N_EP] - ep * EXP_DEV
        for i in range(FF // BLOCK):
            at = slice(i * BLOCK, (i + 1) * BLOCK)
            sel[at, :] = jnp.where(wanted == 0, dq[0, at, :], dq[1, at, :])
        sel_s[...] = jnp.zeros_like(sel_s)
        sel_s[0:FF // BLOCK, 0:D // BLOCK] = jnp.where(wanted == 0, ds[0], ds[1])
        mv_scale().start()

    barrier = pltpu.get_barrier_semaphore()
    partners = (
        at_x(1), at_x(-1), at_x(2), at_z(1), at_z(-1), at_z(2), at_z(-2), other,
        at_y(y_up), at_y(y_dn), at_y(y_op),
    )
    for dev in partners:
        pl.semaphore_signal(barrier, inc=1, device_id=dev, device_id_type=MESH)

    loads = [
        pltpu.make_async_copy(a, b, w_sem.at[i])
        for i, (a, b) in enumerate(((gq_hbm, gq), (uq_hbm, uq), (dq_hbm, dq)))
    ]
    for load in loads:
        load.start()
    own = c * NZ * NX + z * NX + x
    mg[own] = routing_values()
    spread_scales()
    for j in range(NCH):
        dense[j, own] = tok[:, j * CW:(j + 1) * CW]
    accg[...] = jnp.zeros_like(accg)
    accu[...] = jnp.zeros_like(accu)
    pl.semaphore_wait(barrier, len(partners))

    def x_begin(j, carry):
        for k in range(3):
            x_start(j, k)
        return carry

    lax.fori_loop(0, NCH, x_begin, 0)

    def n_copy(k, sent):
        to = (y_up, y_dn, y_op)[k]
        b = cntbuf.at[y if sent else (y_dn, y_up, y_op)[k]]
        return remote(b, b, n_s.at[k], n_r.at[k], at_y(to))

    def rows_of(i):
        return mg[pl.ds(i * 8, 8)].reshape(BLOCK, BLOCK).astype(F32)

    def fill_slots():
        lane = lax.broadcasted_iota(jnp.int32, (BLOCK, BLOCK), 1)
        slot0 = (ep * (EXP_DEV + 1)).astype(F32)
        fills = jnp.zeros((BLOCK, N_EP * NY), F32)
        for i in range(PLANE // BLOCK):
            m = rows_of(i)
            keyed = (lane >= 2 * TOPK) & (lane < 3 * TOPK)
            tally = jnp.zeros((BLOCK, BLOCK), F32)
            for s in range(EXP_DEV + 1):
                n = jnp.sum(jnp.where(keyed & (m == slot0 + s), 1.0, 0.0), axis=1, keepdims=True)
                tally = tally + jnp.where(lane == s, n, 0.0)
            r = lax.broadcasted_iota(jnp.int32, (BLOCK, N_EP * NY), 0) + i * BLOCK
            col = lax.broadcasted_iota(jnp.int32, (BLOCK, N_EP * NY), 1)
            b = r >> 4
            source = (b & 3) * (NZ * NC) + ((b >> 2) & 7) * NC + (b >> 5)
            mine = (col == source * NY + y).astype(BF16)
            fills = fills + jnp.dot(jnp.transpose(tally).astype(BF16), mine, preferred_element_type=F32)
        cntbuf[y] = fills[0:8]
        for k in range(3):
            n_copy(k, True).start()

    def routes():
        lane = lax.broadcasted_iota(jnp.int32, (BLOCK, BLOCK), 1)
        row = lax.broadcasted_iota(jnp.int32, (BLOCK, BLOCK), 0)
        before = (lane < row).astype(BF16)
        first = (ep * EXP_DEV).astype(F32)
        sofar = jnp.zeros((1, BLOCK), F32)
        wsum = jnp.zeros((SLOTS, 1), F32)
        for i in range(PLANE // BLOCK):
            m = rows_of(i)
            gates = pltpu.roll(m, BLOCK - TOPK, 1)
            is_id = lane < TOPK
            den = jnp.sum(jnp.where(is_id, gates, 0.0), axis=1, keepdims=True)
            flags, weights = [], []
            for e in range(EXP_DEV):
                hit = is_id & (m == first + e)
                flags.append(jnp.sum(jnp.where(hit, 1.0, 0.0), axis=1, keepdims=True))
                weights.append(jnp.sum(jnp.where(hit, gates, 0.0), axis=1, keepdims=True) / den)
            flag = jnp.where(lane == 0, flags[0], jnp.where(lane == 1, flags[1], 0.0))
            place = jnp.dot(before, flag.astype(BF16), preferred_element_type=F32) + sofar
            sofar = sofar + jnp.sum(flag, axis=0, keepdims=True)
            spread = []
            for e in range(EXP_DEV):
                at = jnp.sum(jnp.where(lane == e, place, 0.0), axis=1, keepdims=True)
                at = at.astype(jnp.int32)
                spread.append(jnp.where((lane == at) & (flags[e] > 0.0), weights[e], 0.0))
            spread = jnp.concatenate(spread, axis=1)
            chosen = jnp.where(spread > 0.0, 1.0, 0.0)
            unpack[i * BLOCK:(i + 1) * BLOCK, :] = chosen.astype(BF16)
            turned = jnp.transpose(spread)
            pack[:, i * BLOCK:(i + 1) * BLOCK] = jnp.where(turned > 0.0, 1.0, 0.0).astype(BF16)
            wsum = wsum + jnp.sum(turned, axis=1, keepdims=True)
        wslot[...] = jnp.broadcast_to(wsum, (SLOTS, BLOCK))

    def weight(q, e, j, s):
        parts = []
        for i in range(RB):
            row = s[e, pl.ds(j * RB + i, 1), :]
            rows = q[e, pl.ds(pl.multiple_of(j * CW + i * BLOCK, BLOCK), BLOCK), :]
            parts.append((rows.astype(F32) * row).astype(BF16))
        return jnp.concatenate(parts, axis=0)

    def stage(t, late, fn):
        j = t - late

        @pl.when((j >= 0) & (j < NCH))
        def _():
            fn(j)

    def i1(j):
        for k in range(3):
            x_recv(j, k)
        for k in range(4):
            z_start(j, k)

    def i2(j):
        z_recv(j, 2)
        z_start(j, 4)
        z_start(j, 6)
        z_recv(j, 3)
        z_start(j, 5)

    def i3(j):
        for k in (0, 1, 4, 5, 6):
            z_recv(j, k)
        c_start(j)

    def i7(j):
        c_recv(j)

        @pl.when(j == 0)
        def _():
            routes()

        full = dense[j].reshape(PLANE, CW)
        xs[j, y] = jnp.dot(pack[...], full, preferred_element_type=F32).astype(BF16)
        g_y(j, 0, True).start()
        g_y(j, 1, True).start()

    def i8(j):
        g_y(j, 0, False).wait_recv()
        g_y(j, 2, True).start()
        g_y(j, 1, False).wait_recv()
        g_y(j, 3, True).start()

    def i9(j):
        @pl.when(j == 0)
        def _():
            loads[0].wait()
            loads[1].wait()

        g_y(j, 2, False).wait_recv()
        g_y(j, 3, False).wait_recv()
        for e in range(EXP_DEV):
            rows = xs[j, :, e * CAP:(e + 1) * CAP, :].reshape(NY * CAP, CW)
            accg[e] += jnp.dot(rows, weight(gq, e, j, grow), preferred_element_type=F32)
            accu[e] += jnp.dot(rows, weight(uq, e, j, urow), preferred_element_type=F32)

    def in_tick(t, carry):
        stage(t, 5, i7)
        stage(t, 4, i3)
        stage(t, 2, i2)
        stage(t, 0, i1)

        @pl.when(t == 6)
        def _():
            select_moved()

        @pl.when(t == 8)
        def _():
            fill_slots()

        stage(t, 6, lambda j: mv(j).start())
        stage(t, 7, i8)
        stage(t, 9, i9)
        return carry

    lax.fori_loop(0, NCH + 9, in_tick, 0)

    for e in range(EXP_DEV):
        v = accg[e]
        hid[e] = (v / (1.0 + jnp.exp(-v)) * accu[e]).astype(BF16)

    def in_done(j, carry):
        for k in range(3):
            x_sent(j, k)
        for k in range(7):
            z_sent(j, k)
        c_sent(j)
        for k in range(4):
            g_y(j, k, True).wait_send()
        return carry

    lax.fori_loop(0, NCH, in_done, 0)
    for k in range(3):
        n_copy(k, False).wait_recv()
    total = (cntbuf[0] + cntbuf[1] + cntbuf[2] + cntbuf[3]) * (1.0 / MOST)
    cnt[0] = total[0:EXP_DEV + 1]

    def o_y(j, k, sent):
        to = (y_up, y_dn)[k % 2]
        if k < 2:
            src = xs.at[j, y_op, pl.ds(k * half, half)]
            dst = ryh.at[j, k]
        else:
            src = xs.at[j, to]
            dst = ryf.at[j, k - 2]
        return remote(src, dst, yo_s.at[j, k], yo_r.at[j, k], at_y(to))

    def o_c(j):
        return remote(cblock(dense.at[j], 1 - c), crecv.at[j], co_s.at[j], co_r.at[j], other)

    z_steps = ((3, 1), (-3, -1), (4, 2), (2, 2), (-2, -2), (1, 1), (-1, -1))

    def o_z(j, k):
        off, hop = z_steps[k]
        return remote(zblock(dense.at[j], c, zat(off)), zrecv.at[j, k],
                      zo_s.at[j, k], zo_r.at[j, k], at_z(hop))

    def o_x(j, k):
        hop = (1, -1, 2)[k]
        return remote(xblock(dense.at[j], c, z, xat(hop)), xrecv.at[j, pl.ds(k, 1)],
                      xo_s.at[j, k], xo_r.at[j, k], at_x(hop))

    def add(a, b):
        return (a.astype(F32) + b.astype(F32)).astype(BF16)

    def add_z(j, k):
        off, hop = z_steps[k]
        o_z(j, k).wait_recv()
        at = pl.ds(c * NZ * NX + zat(off - hop) * NX, NX)
        dense[j, at] = add(dense[j, at], zrecv[j, k])

    def o0(j):
        cols = pl.ds(pl.multiple_of(j * CW, CW), CW)
        for e in range(EXP_DEV):
            parts = []
            for r in range(FF // BLOCK):
                row = drow[e, r:r + 1, cols]
                rows = dq[e, r * BLOCK:(r + 1) * BLOCK, cols]
                parts.append((rows.astype(F32) * row).astype(BF16))
            w = jnp.concatenate(parts, axis=0)
            out = jnp.dot(hid[e], w, preferred_element_type=F32).astype(BF16)
            xs[j, :, e * CAP:(e + 1) * CAP, :] = out.reshape(NY, CAP, CW)
        o_y(j, 0, True).start()
        o_y(j, 1, True).start()

    def o1(j):
        for k in range(2):
            o_y(j, k, False).wait_recv()
            to = (y_up, y_dn)[k]
            at = pl.ds(k * half, half)
            xs[j, to, at] = add(xs[j, to, at], ryh[j, k])
            o_y(j, 2 + k, True).start()

    def o2(j):
        o_y(j, 2, False).wait_recv()
        o_y(j, 3, False).wait_recv()
        total = xs[j, y].astype(F32) + ryf[j, 0].astype(F32) + ryf[j, 1].astype(F32)
        scaled = (total * wslot[:, 0:1]).astype(BF16)
        n = 256
        for i in range(PLANE // n):
            out = jnp.dot(unpack[i * n:(i + 1) * n, :], scaled, preferred_element_type=F32)
            dense[j, i * (n // ROWS):(i + 1) * (n // ROWS)] = out.astype(BF16).reshape(n // ROWS, ROWS, CW)
        o_c(j).start()

    def o3(j):
        o_c(j).wait_recv()
        at = pl.ds(c * NZ * NX, NZ * NX)
        dense[j, at] = add(dense[j, at], crecv[j])
        for k in (2, 0, 1, 5, 6):
            o_z(j, k).start()

    def o4(j):
        for k in range(3):
            add_z(j, k)
        o_z(j, 3).start()
        o_z(j, 4).start()

    def o5(j):
        for k in range(3, 7):
            o_z(j, k).wait_recv()
        at = pl.ds(c * NZ * NX + z * NX, NX)
        total = dense[j, at].astype(F32)
        for k in range(3, 7):
            total = total + zrecv[j, k].astype(F32)
        dense[j, at] = total.astype(BF16)
        for k in range(3):
            o_x(j, k).start()

    def o6(j):
        total = dense[j, own].astype(F32)
        for k in range(3):
            o_x(j, k).wait_recv()
            total = total + xrecv[j, k].astype(F32)
        comb[:, pl.ds(pl.multiple_of(j * CW, CW), CW)] = total.astype(BF16)

    def out_tick(t, carry):
        stage(t, 0, o0)
        stage(t, 2, o1)
        stage(t, 5, o3)
        stage(t, 7, o4)
        stage(t, 9, o5)
        stage(t, 11, o6)
        stage(t, 4, o2)
        return carry

    lax.fori_loop(0, NCH + 11, out_tick, 0)

    def out_done(j, carry):
        for k in range(4):
            o_y(j, k, True).wait_send()
        o_c(j).wait_send()
        for k in range(7):
            o_z(j, k).wait_send()
        for k in range(3):
            o_x(j, k).wait_send()
        return carry

    lax.fori_loop(0, NCH, out_done, 0)
    for k in range(3):
        n_copy(k, True).wait_send()
    mv(None).wait()
    mv_scale().wait()
    moved_s[0] = got_s[0:FF // BLOCK, 0:D // BLOCK]


def layer(*args):
    vmem = pl.BlockSpec(memory_space=pltpu.VMEM)
    smem = pl.BlockSpec(memory_space=pltpu.SMEM)
    hbm = pl.BlockSpec(memory_space=pl.ANY)
    dma = pltpu.SemaphoreType.DMA
    blocks = NC * NZ * NX
    return pl.pallas_call(
        kernel,
        out_shape=(
            jax.ShapeDtypeStruct((ROWS, D), BF16),
            jax.ShapeDtypeStruct((1, EXP_DEV + 1, N_EP * NY), F32),
            jax.ShapeDtypeStruct((1, FF, D), BF16),
            jax.ShapeDtypeStruct((1, FF // BLOCK, D // BLOCK), BF16),
        ),
        in_specs=[vmem] * 4 + [smem] + [vmem] * 3 + [hbm] * 3,
        out_specs=(vmem, vmem, hbm, vmem),
        scratch_shapes=[
            pltpu.VMEM((NCH, blocks, ROWS, CW), BF16),
            pltpu.VMEM((blocks, ROWS, BLOCK), BF16),
            pltpu.VMEM((NCH, NY, SLOTS, CW), BF16),
            pltpu.VMEM((EXP_DEV, D, FF), BF16),
            pltpu.VMEM((EXP_DEV, D, FF), BF16),
            pltpu.VMEM((EXP_DEV, FF, D), BF16),
            pltpu.VMEM((EXP_DEV, NY * CAP, FF), F32),
            pltpu.VMEM((EXP_DEV, NY * CAP, FF), F32),
            pltpu.VMEM((EXP_DEV, NY * CAP, FF), BF16),
            pltpu.VMEM((NCH, 2, SLOTS // 2, CW), BF16),
            pltpu.VMEM((NCH, 2, SLOTS, CW), BF16),
            pltpu.VMEM((NCH, blocks // 2, ROWS, CW), BF16),
            pltpu.VMEM((NCH, 7, NX, ROWS, CW), BF16),
            pltpu.VMEM((NCH, 3, ROWS, CW), BF16),
            pltpu.VMEM((SLOTS, PLANE), BF16),
            pltpu.VMEM((PLANE, SLOTS), BF16),
            pltpu.VMEM((SLOTS, BLOCK), F32),
            pltpu.VMEM((NY, 8, N_EP * NY), F32),
            pltpu.VMEM((FF, D), BF16),
            pltpu.VMEM((ROWS, BLOCK), BF16),
            pltpu.VMEM((ROWS, BLOCK), BF16),
            pltpu.VMEM((EXP_DEV, D // BLOCK, FF), F32),
            pltpu.VMEM((EXP_DEV, D // BLOCK, FF), F32),
            pltpu.VMEM((EXP_DEV, FF // BLOCK, D), F32),
            dma((3,)),
            dma((2,)), dma((2,)),
            dma((NCH, 3)), dma((NCH, 3)),
            dma((NCH, 7)), dma((NCH, 7)),
            dma((NCH,)), dma((NCH,)),
            dma((NCH, 4)), dma((NCH, 4)),
            dma((11,)), dma((11,)),
            dma((NCH, 4)), dma((NCH, 4)),
            dma((NCH,)), dma((NCH,)),
            dma((NCH, 7)), dma((NCH, 7)),
            dma((NCH, 3)), dma((NCH, 3)),
            dma((3,)), dma((3,)),
        ],
        compiler_params=pltpu.CompilerParams(
            collective_id=0, has_side_effects=True, vmem_limit_bytes=60 * 1024 * 1024
        ),
        cost_estimate=pl.CostEstimate(
            flops=6_000_000_000, bytes_accessed=400_000_000, transcendentals=0
        ),
    )(*args)


def per_device(
    tokens, top_ids, gate_int, replica_pick, plan,
    gate_q, gate_scale, up_q, up_scale, down_q, down_scale,
):
    return layer(
        tokens, top_ids.T, gate_int.T, replica_pick.T, plan,
        gate_scale.transpose(0, 2, 1), up_scale.transpose(0, 2, 1), down_scale,
        gate_q, up_q, down_q,
    )


def solution(mesh):
    return jax.shard_map(
        per_device,
        mesh=mesh,
        in_specs=(
            P(("ep", "dp"), None),
            P(("ep", "dp"), None),
            P(("ep", "dp"), None),
            P(("ep", "dp"), None),
            P(),
            P("ep", None, "dp"),
            P("ep", None, "dp"),
            P("ep", None, "dp"),
            P("ep", None, "dp"),
            P("ep", "dp", None),
            P("ep", "dp", None),
        ),
        out_specs=(
            P(("ep", "dp"), None),
            P("ep", None, None),
            P("ep", "dp", None),
            P("ep", "dp", None),
        ),
        check_vma=False,
    )
```

```python
import functools

import jax
import jax.numpy as jnp
from jax import lax
from jax.experimental import pallas as pl
from jax.experimental.pallas import tpu as pltpu
from jax.sharding import PartitionSpec as P

NX, NZ, NC, NY = 4, 8, 2, 4
N_EP = NX * NZ * NC
ROWS = 16
TOPK = 8
EXP_DEV = 2
MOST = 2
CAP = N_EP * MOST
SLOTS = EXP_DEV * CAP
PLANE = N_EP * ROWS
D = 3584
FF = 256
BLOCK = 128
CW = 256
NCH = D // CW
NB = 2
NA = NCH - NB
RB = CW // BLOCK
F32 = jnp.float32
BF16 = jnp.bfloat16
MESH = pl.DeviceIdType.MESH


def kernel(
    tok, ids_t, gates_t, picks_t, plan, gs, us, ds, gq_hbm, uq_hbm, dq_hbm,
    comb, cnt, moved, moved_s,
    dense, mg, xs, gq, uq, dq, accg, accu, hid, ryh, ryf, crecv, zrecv, xrecv,
    pack, unpack, wslot, cntbuf, sel, sel_s, got_s, grow, urow, drow,
    rt, bd, brc, brx, brz, bry,
    w_sem, mv_s, mv_r, xi_s, xi_r, zi_s, zi_r, ci_s, ci_r, yi_s, yi_r, m_s, m_r,
    yo_s, yo_r, co_s, co_r, zo_s, zo_r, xo_s, xo_r, n_s, n_r,
    rt_s, rt_r, bi_s, bi_r, bo_s, bo_r,
):
    ep = lax.axis_index("ep")
    y = lax.axis_index("dp")
    c = ep % NC
    z = (ep // NC) % NZ
    x = ep // (NC * NZ)
    way = 1 - 2 * c
    y_up, y_dn, y_op = (y + 1) % NY, (y + NY - 1) % NY, (y + 2) % NY

    def zat(k):
        return (z + way * k + 2 * NZ) % NZ

    def xat(k):
        return (x + way * k + 2 * NX) % NX

    def at_x(k):
        return {"ep": (xat(k) * NZ + z) * NC + c, "dp": y}

    def at_z(k):
        return {"ep": (x * NZ + zat(k)) * NC + c, "dp": y}

    def at_y(to):
        return {"ep": ep, "dp": to}

    other = {"ep": (x * NZ + z) * NC + 1 - c, "dp": y}

    def remote(src, dst, ssem, rsem, dev):
        return pltpu.make_async_remote_copy(
            src_ref=src, dst_ref=dst, send_sem=ssem, recv_sem=rsem,
            device_id=dev, device_id_type=MESH,
        )

    def xblock(ref, core, zz, xx):
        return ref.at[pl.ds(core * NZ * NX + zz * NX + xx, 1)]

    def zblock(ref, core, zz):
        return ref.at[pl.ds(core * NZ * NX + zz * NX, NX)]

    def cblock(ref, core):
        return ref.at[pl.ds(core * NZ * NX, NZ * NX)]

    def g_x(ref, ss, rs, k, sent):
        hop = (1, -1, 2)[k]
        b = xblock(ref, c, z, xat(0 if sent else -hop))
        return remote(b, b, ss, rs, at_x(hop))

    def g_z(ref, ss, rs, k, sent):
        off, hop = ((0, 1), (0, -1), (0, 2), (0, -2), (-2, 1), (2, -1), (-2, 2))[k]
        if not sent:
            off = off - hop
        b = zblock(ref, c, zat(off))
        return remote(b, b, ss, rs, at_z(hop))

    def g_c(ref, ss, rs, core):
        b = cblock(ref, core)
        return remote(b, b, ss, rs, other)

    def both(j, fn):
        @pl.when(j == 0)
        def _():
            fn(mg, (m_s.at[pl.ds(0, 3)], m_r.at[pl.ds(0, 3)], m_s.at[pl.ds(3, 7)],
                    m_r.at[pl.ds(3, 7)], m_s.at[10], m_r.at[10]))

        fn(dense.at[j], (xi_s.at[j], xi_r.at[j], zi_s.at[j], zi_r.at[j], ci_s.at[j], ci_r.at[j]))

    def x_start(j, k):
        both(j, lambda ref, q: g_x(ref, q[0].at[k], q[1].at[k], k, True).start())

    def x_recv(j, k):
        both(j, lambda ref, q: g_x(ref, q[0].at[k], q[1].at[k], k, False).wait_recv())

    def x_sent(j, k):
        both(j, lambda ref, q: g_x(ref, q[0].at[k], q[1].at[k], k, True).wait_send())

    def z_start(j, k):
        both(j, lambda ref, q: g_z(ref, q[2].at[k], q[3].at[k], k, True).start())

    def z_recv(j, k):
        both(j, lambda ref, q: g_z(ref, q[2].at[k], q[3].at[k], k, False).wait_recv())

    def z_sent(j, k):
        both(j, lambda ref, q: g_z(ref, q[2].at[k], q[3].at[k], k, True).wait_send())

    def c_start(j):
        both(j, lambda ref, q: g_c(ref, q[4], q[5], c).start())

    def c_recv(j):
        both(j, lambda ref, q: g_c(ref, q[4], q[5], 1 - c).wait_recv())

    def c_sent(j):
        both(j, lambda ref, q: g_c(ref, q[4], q[5], c).wait_send())

    half = SLOTS // 2

    def g_y(j, k, sent):
        if k < 2:
            to = (y_up, y_dn)[k]
            b = xs.at[j, y if sent else (y_dn, y_up)[k]]
        else:
            to = (y_up, y_dn)[k - 2]
            plane = (y_dn, y_up)[k - 2] if sent else y_op
            b = xs.at[j, plane, pl.ds((k - 2) * half, half)]
        return remote(b, b, yi_s.at[j, k], yi_r.at[j, k], at_y(to))

    z_gather = ((0, 1), (0, -1), (0, 2), (0, -2), (-2, 1), (2, -1), (-2, 2))
    y_to = (y_up, y_dn, y_op)
    y_from = (y_dn, y_up, y_op)

    def b_in(i, k, sent):
        if k < 3:
            b, dev = bd.at[i, c, z, x, y if sent else y_from[k]], at_y(y_to[k])
        elif k < 10:
            off, hop = z_gather[k - 3]
            b, dev = bd.at[i, c, zat(off if sent else off - hop), x], at_z(hop)
        elif k < 13:
            hop = (1, -1, 2)[k - 10]
            b, dev = bd.at[i, c, :, xat(0 if sent else -hop)], at_x(hop)
        else:
            b, dev = bd.at[i, c if sent else 1 - c], other
        return remote(b, b, bi_s.at[i, k], bi_r.at[i, k], dev)

    z_scatter = ((3, 1), (-3, -1), (4, 2), (2, 2), (-2, -2), (1, 1), (-1, -1))

    def b_out(i, k):
        if k < 3:
            src, dst, dev = bd.at[i, c, z, x, y_to[k]], bry.at[i, k], at_y(y_to[k])
        elif k < 10:
            off, hop = z_scatter[k - 3]
            src, dst, dev = bd.at[i, c, zat(off), x], brz.at[i, k - 3], at_z(hop)
        elif k < 13:
            hop = (1, -1, 2)[k - 10]
            src, dst, dev = bd.at[i, c, :, xat(hop)], brx.at[i, k - 10], at_x(hop)
        else:
            src, dst, dev = bd.at[i, 1 - c], brc.at[i], other
        return remote(src, dst, bo_s.at[i, k], bo_r.at[i, k], dev)

    def rt_copy(k, sent):
        b = rt.at[y if sent else y_from[k]]
        return remote(b, b, rt_s.at[k], rt_r.at[k], at_y(y_to[k]))

    def routing_values():
        ids = ids_t[...]
        planned = ids == plan[0]
        for r in range(1, N_EP):
            planned = planned | (ids == plan[r])
        there = planned & (picks_t[...] == 1)
        home = ids >> 1
        target = jnp.where(there, (home + N_EP // 2) & (N_EP - 1), home)
        key = target * (EXP_DEV + 1) + jnp.where(there, EXP_DEV, ids & 1)
        cols = jnp.concatenate([ids, gates_t[...], key], axis=0).astype(F32).astype(BF16)
        n = 3 * TOPK
        place = lax.broadcasted_iota(jnp.int32, (n, BLOCK), 0) == lax.broadcasted_iota(jnp.int32, (n, BLOCK), 1)
        return lax.dot_general(
            cols, place.astype(BF16), (((0,), (0,)), ((), ())), preferred_element_type=F32
        ).astype(BF16)

    def spread_scales():
        side = lax.broadcasted_iota(jnp.int32, (2, FF), 0) == lax.broadcasted_iota(jnp.int32, (2, FF), 1) // BLOCK
        n = D // BLOCK
        wide = lax.broadcasted_iota(jnp.int32, (n, D), 0) == lax.broadcasted_iota(jnp.int32, (n, D), 1) // BLOCK
        for e in range(EXP_DEV):
            for src, dst in ((gs, grow), (us, urow)):
                dst[e] = lax.dot_general(
                    src[e], side.astype(BF16), (((0,), (0,)), ((), ())), preferred_element_type=F32
                )
            drow[e] = jnp.dot(ds[e], wide.astype(BF16), preferred_element_type=F32)

    def mv(j):
        cols = slice(None) if j is None else pl.ds(pl.multiple_of(j * CW, CW), CW)
        return remote(sel.at[:, cols], moved.at[0, :, cols], mv_s.at[0], mv_r.at[0], at_x(2))

    def mv_scale():
        return remote(sel_s, got_s, mv_s.at[1], mv_r.at[1], at_x(2))

    def select_moved():
        loads[2].wait()
        wanted = plan[(ep + N_EP // 2) % N_EP] - ep * EXP_DEV
        for i in range(FF // BLOCK):
            at = slice(i * BLOCK, (i + 1) * BLOCK)
            sel[at, :] = jnp.where(wanted == 0, dq[0, at, :], dq[1, at, :])
        sel_s[...] = jnp.zeros_like(sel_s)
        sel_s[0:FF // BLOCK, 0:D // BLOCK] = jnp.where(wanted == 0, ds[0], ds[1])
        mv_scale().start()

    barrier = pltpu.get_barrier_semaphore()
    partners = (
        at_x(1), at_x(-1), at_x(2), at_z(1), at_z(-1), at_z(2), at_z(-2), other,
        at_y(y_up), at_y(y_dn), at_y(y_op),
    )
    for dev in partners:
        pl.semaphore_signal(barrier, inc=1, device_id=dev, device_id_type=MESH)

    loads = [
        pltpu.make_async_copy(a, b, w_sem.at[i])
        for i, (a, b) in enumerate(((gq_hbm, gq), (uq_hbm, uq), (dq_hbm, dq)))
    ]
    for load in loads:
        load.start()
    own = c * NZ * NX + z * NX + x
    mg[own] = routing_values()
    spread_scales()
    for j in range(NA):
        dense[j, own] = tok[:, j * CW:(j + 1) * CW]
    for i in range(NB):
        bd[i, c, z, x, y] = tok[:, (NA + i) * CW:(NA + i + 1) * CW]
    rt[y] = jnp.zeros((8, PLANE), F32)
    accg[...] = jnp.zeros_like(accg)
    accu[...] = jnp.zeros_like(accu)
    pl.semaphore_wait(barrier, len(partners))

    def x_begin(j, carry):
        for k in range(3):
            x_start(j, k)
        return carry

    lax.fori_loop(0, NA, x_begin, 0)
    for i in range(NB):
        for k in range(3):
            b_in(i, k, True).start()

    def n_copy(k, sent):
        to = (y_up, y_dn, y_op)[k]
        b = cntbuf.at[y if sent else (y_dn, y_up, y_op)[k]]
        return remote(b, b, n_s.at[k], n_r.at[k], at_y(to))

    def rows_of(i):
        return mg[pl.ds(i * 8, 8)].reshape(BLOCK, BLOCK).astype(F32)

    def fill_slots():
        lane = lax.broadcasted_iota(jnp.int32, (BLOCK, BLOCK), 1)
        slot0 = (ep * (EXP_DEV + 1)).astype(F32)
        fills = jnp.zeros((BLOCK, N_EP * NY), F32)
        for i in range(PLANE // BLOCK):
            m = rows_of(i)
            keyed = (lane >= 2 * TOPK) & (lane < 3 * TOPK)
            tally = jnp.zeros((BLOCK, BLOCK), F32)
            for s in range(EXP_DEV + 1):
                n = jnp.sum(jnp.where(keyed & (m == slot0 + s), 1.0, 0.0), axis=1, keepdims=True)
                tally = tally + jnp.where(lane == s, n, 0.0)
            r = lax.broadcasted_iota(jnp.int32, (BLOCK, N_EP * NY), 0) + i * BLOCK
            col = lax.broadcasted_iota(jnp.int32, (BLOCK, N_EP * NY), 1)
            b = r >> 4
            source = (b & 3) * (NZ * NC) + ((b >> 2) & 7) * NC + (b >> 5)
            mine = (col == source * NY + y).astype(BF16)
            fills = fills + jnp.dot(jnp.transpose(tally).astype(BF16), mine, preferred_element_type=F32)
        cntbuf[y] = fills[0:8]
        for k in range(3):
            n_copy(k, True).start()

    def routes():
        lane = lax.broadcasted_iota(jnp.int32, (BLOCK, BLOCK), 1)
        row = lax.broadcasted_iota(jnp.int32, (BLOCK, BLOCK), 0)
        before = (lane < row).astype(BF16)
        first = (ep * EXP_DEV).astype(F32)
        sofar = jnp.zeros((1, BLOCK), F32)
        wsum = jnp.zeros((SLOTS, 1), F32)
        for i in range(PLANE // BLOCK):
            m = rows_of(i)
            gates = pltpu.roll(m, BLOCK - TOPK, 1)
            is_id = lane < TOPK
            den = jnp.sum(jnp.where(is_id, gates, 0.0), axis=1, keepdims=True)
            flags, weights = [], []
            for e in range(EXP_DEV):
                hit = is_id & (m == first + e)
                flags.append(jnp.sum(jnp.where(hit, 1.0, 0.0), axis=1, keepdims=True))
                weights.append(jnp.sum(jnp.where(hit, gates, 0.0), axis=1, keepdims=True) / den)
            flag = jnp.where(lane == 0, flags[0], jnp.where(lane == 1, flags[1], 0.0))
            place = jnp.dot(before, flag.astype(BF16), preferred_element_type=F32) + sofar
            sofar = sofar + jnp.sum(flag, axis=0, keepdims=True)
            spread = []
            for e in range(EXP_DEV):
                at = jnp.sum(jnp.where(lane == e, place, 0.0), axis=1, keepdims=True)
                at = at.astype(jnp.int32)
                spread.append(jnp.where((lane == at) & (flags[e] > 0.0), weights[e], 0.0))
            spread = jnp.concatenate(spread, axis=1)
            chosen = jnp.where(spread > 0.0, 1.0, 0.0)
            unpack[i * BLOCK:(i + 1) * BLOCK, :] = chosen.astype(BF16)
            turned = jnp.transpose(spread)
            here = jnp.where(turned > 0.0, 1.0, 0.0)
            at = slice(i * BLOCK, (i + 1) * BLOCK)
            pack[y, :, at] = here.astype(BF16)
            wsum = wsum + jnp.sum(turned, axis=1, keepdims=True)
            for e in range(EXP_DEV):
                part = slice(e * CAP, (e + 1) * CAP)
                number = here[part] * (row + 1).astype(F32)
                rt[y, e:e + 1, at] = jnp.sum(number, axis=0, keepdims=True)
                rt[y, EXP_DEV + e:EXP_DEV + e + 1, at] = jnp.sum(turned[part], axis=0, keepdims=True)
        wslot[y] = jnp.broadcast_to(wsum, (SLOTS, BLOCK))
        for k in range(3):
            rt_copy(k, True).start()

    def other_plane(k):
        p = y_from[k]
        rt_copy(k, False).wait_recv()
        n = 2 * BLOCK
        slot = (lax.broadcasted_iota(jnp.int32, (CAP, n), 0) + 1).astype(F32)
        for e in range(EXP_DEV):
            part = slice(e * CAP, (e + 1) * CAP)
            wsum = jnp.zeros((CAP, 1), F32)
            for i in range(PLANE // n):
                at = slice(i * n, (i + 1) * n)
                here = slot == rt[p, e:e + 1, at]
                pack[p, part, at] = jnp.where(here, 1.0, 0.0).astype(BF16)
                weights = jnp.where(here, rt[p, EXP_DEV + e:EXP_DEV + e + 1, at], 0.0)
                wsum = wsum + jnp.sum(weights, axis=1, keepdims=True)
            wslot[p, part] = jnp.broadcast_to(wsum, (CAP, BLOCK))

    def weight(q, e, j, s):
        parts = []
        for i in range(RB):
            row = s[e, pl.ds(j * RB + i, 1), :]
            rows = q[e, pl.ds(pl.multiple_of(j * CW + i * BLOCK, BLOCK), BLOCK), :]
            parts.append((rows.astype(F32) * row).astype(BF16))
        return jnp.concatenate(parts, axis=0)

    def stage(t, late, fn, n=NA):
        j = t - late

        @pl.when((j >= 0) & (j < n))
        def _():
            fn(j)

    def i1(j):
        for k in range(3):
            x_recv(j, k)
        for k in (2, 3, 0, 1):
            z_start(j, k)

    def i2(j):
        z_recv(j, 2)
        z_start(j, 4)
        z_start(j, 6)
        z_recv(j, 3)
        z_start(j, 5)

    def i3(j):
        for k in (0, 1, 4, 5, 6):
            z_recv(j, k)
        c_start(j)

    def i7(j):
        c_recv(j)

        @pl.when(j == 0)
        def _():
            routes()

        full = dense[j].reshape(PLANE, CW)
        xs[j, y] = jnp.dot(pack[y], full, preferred_element_type=F32).astype(BF16)
        g_y(j, 0, True).start()
        g_y(j, 1, True).start()

    def i8(j):
        g_y(j, 0, False).wait_recv()
        g_y(j, 2, True).start()
        g_y(j, 1, False).wait_recv()
        g_y(j, 3, True).start()

    def first_layer(j):
        for e in range(EXP_DEV):
            rows = xs[j, :, e * CAP:(e + 1) * CAP, :].reshape(NY * CAP, CW)
            accg[e] += jnp.dot(rows, weight(gq, e, j, grow), preferred_element_type=F32)
            accu[e] += jnp.dot(rows, weight(uq, e, j, urow), preferred_element_type=F32)

    def i9(j):
        @pl.when(j == 0)
        def _():
            loads[0].wait()
            loads[1].wait()

        g_y(j, 2, False).wait_recv()
        g_y(j, 3, False).wait_recv()
        first_layer(j)

    def b1(i):
        for k in range(3):
            b_in(i, k, False).wait_recv()
        for k in (5, 6, 3, 4):
            b_in(i, k, True).start()

    def b2(i):
        b_in(i, 5, False).wait_recv()
        b_in(i, 6, False).wait_recv()
        for k in (9, 7, 8):
            b_in(i, k, True).start()

    def b3(i):
        for k in (3, 4, 7, 8, 9):
            b_in(i, k, False).wait_recv()
        for k in (10, 11, 12):
            b_in(i, k, True).start()

    def b4(i):
        for k in (10, 11, 12):
            b_in(i, k, False).wait_recv()
        b_in(i, 13, True).start()

    def b5(i):
        b_in(i, 13, False).wait_recv()
        for p in range(NY):
            rows = bd[i, :, :, :, p].reshape(PLANE, CW)
            xs[NA + i, p] = jnp.dot(pack[p], rows, preferred_element_type=F32).astype(BF16)
        first_layer(NA + i)

    def in_tick(t, carry):
        stage(t, 5, i7)
        stage(t, 4, i3)
        stage(t, 2, i2)
        stage(t, 0, i1)

        @pl.when(t == 1)
        def _():
            select_moved()

        @pl.when(t == 8)
        def _():
            fill_slots()

        @pl.when((t >= 1) & (t < 8))
        def _():
            mv(2 * t - 2).start()
            mv(2 * t - 1).start()

        stage(t, 7, i8)
        stage(t, 9, i9)
        stage(t, 10, lambda _: other_plane(0), 1)
        stage(t, 11, lambda _: other_plane(1), 1)
        stage(t, 12, lambda _: other_plane(2), 1)
        stage(t, 3, b1, NB)
        stage(t, 5, b2, NB)
        stage(t, 7, b3, NB)
        stage(t, 15, b4, NB)
        stage(t, 16, b5, NB)
        return carry

    lax.fori_loop(0, NA + 9, in_tick, 0)

    for e in range(EXP_DEV):
        v = accg[e]
        hid[e] = (v / (1.0 + jnp.exp(-v)) * accu[e]).astype(BF16)

    def in_done(j, carry):
        for k in range(3):
            x_sent(j, k)
        for k in range(7):
            z_sent(j, k)
        c_sent(j)
        for k in range(4):
            g_y(j, k, True).wait_send()
        return carry

    lax.fori_loop(0, NA, in_done, 0)

    def b_in_done(i, carry):
        for k in range(14):
            b_in(i, k, True).wait_send()
        return carry

    lax.fori_loop(0, NB, b_in_done, 0)
    for k in range(3):
        n_copy(k, False).wait_recv()
    total = (cntbuf[0] + cntbuf[1] + cntbuf[2] + cntbuf[3]) * (1.0 / MOST)
    cnt[0] = total[0:EXP_DEV + 1]

    def o_y(j, k, sent):
        to = (y_up, y_dn)[k % 2]
        if k < 2:
            src = xs.at[j, y_op, pl.ds(k * half, half)]
            dst = ryh.at[j, k]
        else:
            src = xs.at[j, to]
            dst = ryf.at[j, k - 2]
        return remote(src, dst, yo_s.at[j, k], yo_r.at[j, k], at_y(to))

    def o_c(j):
        return remote(cblock(dense.at[j], 1 - c), crecv.at[j], co_s.at[j], co_r.at[j], other)

    z_steps = ((3, 1), (-3, -1), (4, 2), (2, 2), (-2, -2), (1, 1), (-1, -1))

    def o_z(j, k):
        off, hop = z_steps[k]
        return remote(zblock(dense.at[j], c, zat(off)), zrecv.at[j, k],
                      zo_s.at[j, k], zo_r.at[j, k], at_z(hop))

    def o_x(j, k):
        hop = (1, -1, 2)[k]
        return remote(xblock(dense.at[j], c, z, xat(hop)), xrecv.at[j, pl.ds(k, 1)],
                      xo_s.at[j, k], xo_r.at[j, k], at_x(hop))

    def add(a, b):
        return (a.astype(F32) + b.astype(F32)).astype(BF16)

    def add_z(j, k):
        off, hop = z_steps[k]
        o_z(j, k).wait_recv()
        at = pl.ds(c * NZ * NX + zat(off - hop) * NX, NX)
        dense[j, at] = add(dense[j, at], zrecv[j, k])

    def second_layer(j):
        cols = pl.ds(pl.multiple_of(j * CW, CW), CW)
        for e in range(EXP_DEV):
            parts = []
            for r in range(FF // BLOCK):
                row = drow[e, r:r + 1, cols]
                rows = dq[e, r * BLOCK:(r + 1) * BLOCK, cols]
                parts.append((rows.astype(F32) * row).astype(BF16))
            w = jnp.concatenate(parts, axis=0)
            out = jnp.dot(hid[e], w, preferred_element_type=F32).astype(BF16)
            xs[j, :, e * CAP:(e + 1) * CAP, :] = out.reshape(NY, CAP, CW)

    def o0(j):
        second_layer(j)
        o_y(j, 0, True).start()
        o_y(j, 1, True).start()

    def o1(j):
        for k in range(2):
            o_y(j, k, False).wait_recv()
            to = (y_up, y_dn)[k]
            at = pl.ds(k * half, half)
            xs[j, to, at] = add(xs[j, to, at], ryh[j, k])
            o_y(j, 2 + k, True).start()

    def o2(j):
        o_y(j, 2, False).wait_recv()
        o_y(j, 3, False).wait_recv()
        total = xs[j, y].astype(F32) + ryf[j, 0].astype(F32) + ryf[j, 1].astype(F32)
        scaled = (total * wslot[y, :, 0:1]).astype(BF16)
        n = 256
        for i in range(PLANE // n):
            out = jnp.dot(unpack[i * n:(i + 1) * n, :], scaled, preferred_element_type=F32)
            dense[j, i * (n // ROWS):(i + 1) * (n // ROWS)] = out.astype(BF16).reshape(n // ROWS, ROWS, CW)
        o_c(j).start()

    def o3(j):
        o_c(j).wait_recv()
        at = pl.ds(c * NZ * NX, NZ * NX)
        dense[j, at] = add(dense[j, at], crecv[j])
        for k in (2, 0, 1, 5, 6):
            o_z(j, k).start()

    def o4(j):
        for k in range(3):
            add_z(j, k)
        o_z(j, 3).start()
        o_z(j, 4).start()

    def o5(j):
        for k in range(3, 7):
            o_z(j, k).wait_recv()
        at = pl.ds(c * NZ * NX + z * NX, NX)
        total = dense[j, at].astype(F32)
        for k in range(3, 7):
            total = total + zrecv[j, k].astype(F32)
        dense[j, at] = total.astype(BF16)
        for k in range(3):
            o_x(j, k).start()

    def o6(j):
        total = dense[j, own].astype(F32)
        for k in range(3):
            o_x(j, k).wait_recv()
            total = total + xrecv[j, k].astype(F32)
        comb[:, pl.ds(pl.multiple_of(j * CW, CW), CW)] = total.astype(BF16)

    def c0(i):
        second_layer(NA + i)
        n = 2 * BLOCK
        for p in range(NY):
            scaled = (xs[NA + i, p].astype(F32) * wslot[p, :, 0:1]).astype(BF16)
            for h in range(NC):
                half_rows = pack[p, :, h * (PLANE // NC):(h + 1) * (PLANE // NC)]
                out = lax.dot_general(
                    half_rows, scaled, (((0,), (0,)), ((), ())), preferred_element_type=F32
                )
                bd[i, h, :, :, p] = out.astype(BF16).reshape(NZ, NX, ROWS, CW)
        b_out(i, 13).start()

    def c1(i):
        b_out(i, 13).wait_recv()
        for zz in range(NZ):
            bd[i, c, zz] = add(bd[i, c, zz], brc[i, zz])
        for k in (10, 11, 12):
            b_out(i, k).start()

    def c2(i):
        for k in (10, 11, 12):
            b_out(i, k).wait_recv()
        for zz in range(NZ):
            total = bd[i, c, zz, x].astype(F32)
            for k in range(3):
                total = total + brx[i, k, zz].astype(F32)
            bd[i, c, zz, x] = total.astype(BF16)
        for k in (5, 3, 4, 8, 9):
            b_out(i, k).start()

    def c3(i):
        for k in range(3):
            off, hop = z_scatter[k]
            b_out(i, 3 + k).wait_recv()
            zz = zat(off - hop)
            bd[i, c, zz, x] = add(bd[i, c, zz, x], brz[i, k])
        b_out(i, 6).start()
        b_out(i, 7).start()

    def c4(i):
        total = bd[i, c, z, x].astype(F32)
        for k in range(3, 7):
            b_out(i, 3 + k).wait_recv()
            total = total + brz[i, k].astype(F32)
        bd[i, c, z, x] = total.astype(BF16)
        for k in range(3):
            b_out(i, k).start()

    def c5(i):
        total = bd[i, c, z, x, y].astype(F32)
        for k in range(3):
            b_out(i, k).wait_recv()
            total = total + bry[i, k].astype(F32)
        comb[:, pl.ds(pl.multiple_of((NA + i) * CW, CW), CW)] = total.astype(BF16)

    def out_tick(t, carry):
        stage(t, 0, o0)
        stage(t, 2, o1)
        stage(t, 5, o3)
        stage(t, 7, o4)
        stage(t, 9, o5)
        stage(t, 11, o6)
        stage(t, 4, o2)


        stage(t, 1, c0, NB)
        stage(t, 3, c1, NB)
        stage(t, 10, c2, NB)
        stage(t, 13, c3, NB)
        stage(t, 15, c4, NB)
        stage(t, 18, c5, NB)
        return carry

    lax.fori_loop(0, NA + 11, out_tick, 0)

    def out_done(j, carry):
        for k in range(4):
            o_y(j, k, True).wait_send()
        o_c(j).wait_send()
        for k in range(7):
            o_z(j, k).wait_send()
        for k in range(3):
            o_x(j, k).wait_send()
        return carry

    lax.fori_loop(0, NA, out_done, 0)

    def b_out_done(i, carry):
        for k in range(14):
            b_out(i, k).wait_send()
        return carry

    lax.fori_loop(0, NB, b_out_done, 0)
    for k in range(3):
        rt_copy(k, True).wait_send()
    for k in range(3):
        n_copy(k, True).wait_send()
    mv(None).wait()
    mv_scale().wait()
    moved_s[0] = got_s[0:FF // BLOCK, 0:D // BLOCK]


def layer(*args):
    vmem = pl.BlockSpec(memory_space=pltpu.VMEM)
    smem = pl.BlockSpec(memory_space=pltpu.SMEM)
    hbm = pl.BlockSpec(memory_space=pl.ANY)
    dma = pltpu.SemaphoreType.DMA
    blocks = NC * NZ * NX
    return pl.pallas_call(
        kernel,
        out_shape=(
            jax.ShapeDtypeStruct((ROWS, D), BF16),
            jax.ShapeDtypeStruct((1, EXP_DEV + 1, N_EP * NY), F32),
            jax.ShapeDtypeStruct((1, FF, D), BF16),
            jax.ShapeDtypeStruct((1, FF // BLOCK, D // BLOCK), BF16),
        ),
        in_specs=[vmem] * 4 + [smem] + [vmem] * 3 + [hbm] * 3,
        out_specs=(vmem, vmem, hbm, vmem),
        scratch_shapes=[
            pltpu.VMEM((NA, blocks, ROWS, CW), BF16),
            pltpu.VMEM((blocks, ROWS, BLOCK), BF16),
            pltpu.VMEM((NCH, NY, SLOTS, CW), BF16),
            pltpu.VMEM((EXP_DEV, D, FF), BF16),
            pltpu.VMEM((EXP_DEV, D, FF), BF16),
            pltpu.VMEM((EXP_DEV, FF, D), BF16),
            pltpu.VMEM((EXP_DEV, NY * CAP, FF), F32),
            pltpu.VMEM((EXP_DEV, NY * CAP, FF), F32),
            pltpu.VMEM((EXP_DEV, NY * CAP, FF), BF16),
            pltpu.VMEM((NA, 2, SLOTS // 2, CW), BF16),
            pltpu.VMEM((NA, 2, SLOTS, CW), BF16),
            pltpu.VMEM((NA, blocks // 2, ROWS, CW), BF16),
            pltpu.VMEM((NA, 7, NX, ROWS, CW), BF16),
            pltpu.VMEM((NA, 3, ROWS, CW), BF16),
            pltpu.VMEM((NY, SLOTS, PLANE), BF16),
            pltpu.VMEM((PLANE, SLOTS), BF16),
            pltpu.VMEM((NY, SLOTS, BLOCK), F32),
            pltpu.VMEM((NY, 8, N_EP * NY), F32),
            pltpu.VMEM((FF, D), BF16),
            pltpu.VMEM((ROWS, BLOCK), BF16),
            pltpu.VMEM((ROWS, BLOCK), BF16),
            pltpu.VMEM((EXP_DEV, D // BLOCK, FF), F32),
            pltpu.VMEM((EXP_DEV, D // BLOCK, FF), F32),
            pltpu.VMEM((EXP_DEV, FF // BLOCK, D), F32),
            pltpu.VMEM((NY, 8, PLANE), F32),
            pltpu.VMEM((NB, NC, NZ, NX, NY, ROWS, CW), BF16),
            pltpu.VMEM((NB, NZ, NX, NY, ROWS, CW), BF16),
            pltpu.VMEM((NB, 3, NZ, NY, ROWS, CW), BF16),
            pltpu.VMEM((NB, 7, NY, ROWS, CW), BF16),
            pltpu.VMEM((NB, 3, ROWS, CW), BF16),
            dma((3,)),
            dma((2,)), dma((2,)),
            dma((NA, 3)), dma((NA, 3)),
            dma((NA, 7)), dma((NA, 7)),
            dma((NA,)), dma((NA,)),
            dma((NA, 4)), dma((NA, 4)),
            dma((11,)), dma((11,)),
            dma((NA, 4)), dma((NA, 4)),
            dma((NA,)), dma((NA,)),
            dma((NA, 7)), dma((NA, 7)),
            dma((NA, 3)), dma((NA, 3)),
            dma((3,)), dma((3,)),
            dma((3,)), dma((3,)),
            dma((NB, 14)), dma((NB, 14)),
            dma((NB, 14)), dma((NB, 14)),
        ],
        compiler_params=pltpu.CompilerParams(
            collective_id=0, has_side_effects=True, vmem_limit_bytes=60 * 1024 * 1024
        ),
        cost_estimate=pl.CostEstimate(
            flops=6_000_000_000, bytes_accessed=400_000_000, transcendentals=0
        ),
    )(*args)


def per_device(
    tokens, top_ids, gate_int, replica_pick, plan,
    gate_q, gate_scale, up_q, up_scale, down_q, down_scale,
):
    return layer(
        tokens, top_ids.T, gate_int.T, replica_pick.T, plan,
        gate_scale.transpose(0, 2, 1), up_scale.transpose(0, 2, 1), down_scale,
        gate_q, up_q, down_q,
    )


def solution(mesh):
    return jax.shard_map(
        per_device,
        mesh=mesh,
        in_specs=(
            P(("ep", "dp"), None),
            P(("ep", "dp"), None),
            P(("ep", "dp"), None),
            P(("ep", "dp"), None),
            P(),
            P("ep", None, "dp"),
            P("ep", None, "dp"),
            P("ep", None, "dp"),
            P("ep", None, "dp"),
            P("ep", "dp", None),
            P("ep", "dp", None),
        ),
        out_specs=(
            P(("ep", "dp"), None),
            P("ep", None, None),
            P("ep", "dp", None),
            P("ep", "dp", None),
        ),
        check_vma=False,
    )
```

```python
import functools

import jax
import jax.numpy as jnp
from jax import lax
from jax.experimental import pallas as pl
from jax.experimental.pallas import tpu as pltpu
from jax.sharding import PartitionSpec as P

NX, NZ, NC, NY = 4, 8, 2, 4
N_EP = NX * NZ * NC
ROWS = 16
TOPK = 8
EXP_DEV = 2
MOST = 2
CAP = N_EP * MOST
SLOTS = EXP_DEV * CAP
PLANE = N_EP * ROWS
D = 3584
FF = 256
BLOCK = 128
CW = 256
NCH = D // CW
NB = 2
NA = NCH - NB
RB = CW // BLOCK
F32 = jnp.float32
BF16 = jnp.bfloat16
MESH = pl.DeviceIdType.MESH


def kernel(
    tok, ids_t, gates_t, picks_t, plan, gs, us, ds, gq_hbm, uq_hbm, dq_hbm,
    comb, cnt, moved, moved_s,
    dense, mg, xs, gq, uq, dq, accg, accu, hid, ryh, ryf, crecv, zrecv, xrecv,
    pack, unpack, wslot, cntbuf, sel, sel_s, got_s, grow, urow, drow,
    rt, shares, bd, brc, brx, brz, bry,
    w_sem, mv_s, mv_r, xi_s, xi_r, zi_s, zi_r, ci_s, ci_r, yi_s, yi_r, m_s, m_r,
    yo_s, yo_r, co_s, co_r, zo_s, zo_r, xo_s, xo_r, n_s, n_r,
    rt_s, rt_r, bi_s, bi_r, bo_s, bo_r,
):
    ep = lax.axis_index("ep")
    y = lax.axis_index("dp")
    c = ep % NC
    z = (ep // NC) % NZ
    x = ep // (NC * NZ)
    way = 1 - 2 * c
    y_up, y_dn, y_op = (y + 1) % NY, (y + NY - 1) % NY, (y + 2) % NY

    def zat(k):
        return (z + way * k + 2 * NZ) % NZ

    def xat(k):
        return (x + way * k + 2 * NX) % NX

    def at_x(k):
        return {"ep": (xat(k) * NZ + z) * NC + c, "dp": y}

    def at_z(k):
        return {"ep": (x * NZ + zat(k)) * NC + c, "dp": y}

    def at_y(to):
        return {"ep": ep, "dp": to}

    other = {"ep": (x * NZ + z) * NC + 1 - c, "dp": y}

    def remote(src, dst, ssem, rsem, dev):
        return pltpu.make_async_remote_copy(
            src_ref=src, dst_ref=dst, send_sem=ssem, recv_sem=rsem,
            device_id=dev, device_id_type=MESH,
        )

    def xblock(ref, core, zz, xx):
        return ref.at[pl.ds(core * NZ * NX + zz * NX + xx, 1)]

    def zblock(ref, core, zz):
        return ref.at[pl.ds(core * NZ * NX + zz * NX, NX)]

    def cblock(ref, core):
        return ref.at[pl.ds(core * NZ * NX, NZ * NX)]

    def g_x(ref, ss, rs, k, sent):
        hop = (1, -1, 2)[k]
        b = xblock(ref, c, z, xat(0 if sent else -hop))
        return remote(b, b, ss, rs, at_x(hop))

    def g_z(ref, ss, rs, k, sent):
        off, hop = ((0, 1), (0, -1), (0, 2), (0, -2), (-2, 1), (2, -1), (-2, 2))[k]
        if not sent:
            off = off - hop
        b = zblock(ref, c, zat(off))
        return remote(b, b, ss, rs, at_z(hop))

    def g_c(ref, ss, rs, core):
        b = cblock(ref, core)
        return remote(b, b, ss, rs, other)

    def both(j, fn):
        @pl.when(j == 0)
        def _():
            fn(mg, (m_s.at[pl.ds(0, 3)], m_r.at[pl.ds(0, 3)], m_s.at[pl.ds(3, 7)],
                    m_r.at[pl.ds(3, 7)], m_s.at[10], m_r.at[10]))

        fn(dense.at[j], (xi_s.at[j], xi_r.at[j], zi_s.at[j], zi_r.at[j], ci_s.at[j], ci_r.at[j]))

    def x_start(j, k):
        both(j, lambda ref, q: g_x(ref, q[0].at[k], q[1].at[k], k, True).start())

    def x_recv(j, k):
        both(j, lambda ref, q: g_x(ref, q[0].at[k], q[1].at[k], k, False).wait_recv())

    def x_sent(j, k):
        both(j, lambda ref, q: g_x(ref, q[0].at[k], q[1].at[k], k, True).wait_send())

    def z_start(j, k):
        both(j, lambda ref, q: g_z(ref, q[2].at[k], q[3].at[k], k, True).start())

    def z_recv(j, k):
        both(j, lambda ref, q: g_z(ref, q[2].at[k], q[3].at[k], k, False).wait_recv())

    def z_sent(j, k):
        both(j, lambda ref, q: g_z(ref, q[2].at[k], q[3].at[k], k, True).wait_send())

    def c_start(j):
        both(j, lambda ref, q: g_c(ref, q[4], q[5], c).start())

    def c_recv(j):
        both(j, lambda ref, q: g_c(ref, q[4], q[5], 1 - c).wait_recv())

    def c_sent(j):
        both(j, lambda ref, q: g_c(ref, q[4], q[5], c).wait_send())

    half = SLOTS // 2

    def g_y(j, k, sent):
        if k < 2:
            to = (y_up, y_dn)[k]
            b = xs.at[j, y if sent else (y_dn, y_up)[k]]
        else:
            to = (y_up, y_dn)[k - 2]
            plane = (y_dn, y_up)[k - 2] if sent else y_op
            b = xs.at[j, plane, pl.ds((k - 2) * half, half)]
        return remote(b, b, yi_s.at[j, k], yi_r.at[j, k], at_y(to))

    z_gather = ((0, 1), (0, -1), (0, 2), (0, -2), (-2, 1), (2, -1), (-2, 2))
    y_to = (y_up, y_dn, y_op)
    y_from = (y_dn, y_up, y_op)

    def b_in(i, k, sent):
        if k < 3:
            b, dev = bd.at[i, c, z, x, y if sent else y_from[k]], at_y(y_to[k])
        elif k < 10:
            off, hop = z_gather[k - 3]
            b, dev = bd.at[i, c, zat(off if sent else off - hop), x], at_z(hop)
        elif k < 13:
            hop = (1, -1, 2)[k - 10]
            b, dev = bd.at[i, c, :, xat(0 if sent else -hop)], at_x(hop)
        else:
            b, dev = bd.at[i, c if sent else 1 - c], other
        return remote(b, b, bi_s.at[i, k], bi_r.at[i, k], dev)

    z_scatter = ((3, 1), (-3, -1), (4, 2), (2, 2), (-2, -2), (1, 1), (-1, -1))

    def b_out(i, k):
        if k < 3:
            src, dst, dev = bd.at[i, c, z, x, y_to[k]], bry.at[i, k], at_y(y_to[k])
        elif k < 10:
            off, hop = z_scatter[k - 3]
            src, dst, dev = bd.at[i, c, zat(off), x], brz.at[i, k - 3], at_z(hop)
        elif k < 13:
            hop = (1, -1, 2)[k - 10]
            src, dst, dev = bd.at[i, c, :, xat(hop)], brx.at[i, k - 10], at_x(hop)
        else:
            src, dst, dev = bd.at[i, 1 - c], brc.at[i], other
        return remote(src, dst, bo_s.at[i, k], bo_r.at[i, k], dev)

    def rt_copy(k, sent):
        b = rt.at[y if sent else y_from[k]]
        return remote(b, b, rt_s.at[k], rt_r.at[k], at_y(y_to[k]))

    def routing_values():
        ids = ids_t[...]
        planned = ids == plan[0]
        for r in range(1, N_EP):
            planned = planned | (ids == plan[r])
        there = planned & (picks_t[...] == 1)
        home = ids >> 1
        target = jnp.where(there, (home + N_EP // 2) & (N_EP - 1), home)
        key = target * (EXP_DEV + 1) + jnp.where(there, EXP_DEV, ids & 1)
        cols = jnp.concatenate([ids, gates_t[...], key], axis=0).astype(F32).astype(BF16)
        n = 3 * TOPK
        place = lax.broadcasted_iota(jnp.int32, (n, BLOCK), 0) == lax.broadcasted_iota(jnp.int32, (n, BLOCK), 1)
        return lax.dot_general(
            cols, place.astype(BF16), (((0,), (0,)), ((), ())), preferred_element_type=F32
        ).astype(BF16)

    def spread_scales():
        side = lax.broadcasted_iota(jnp.int32, (2, FF), 0) == lax.broadcasted_iota(jnp.int32, (2, FF), 1) // BLOCK
        n = D // BLOCK
        wide = lax.broadcasted_iota(jnp.int32, (n, D), 0) == lax.broadcasted_iota(jnp.int32, (n, D), 1) // BLOCK
        for e in range(EXP_DEV):
            for src, dst in ((gs, grow), (us, urow)):
                dst[e] = lax.dot_general(
                    src[e], side.astype(BF16), (((0,), (0,)), ((), ())), preferred_element_type=F32
                )
            drow[e] = jnp.dot(ds[e], wide.astype(BF16), preferred_element_type=F32)

    def mv(j):
        cols = slice(None) if j is None else pl.ds(pl.multiple_of(j * CW, CW), CW)
        return remote(sel.at[:, cols], moved.at[0, :, cols], mv_s.at[0], mv_r.at[0], at_x(2))

    def mv_scale():
        return remote(sel_s, got_s, mv_s.at[1], mv_r.at[1], at_x(2))

    def select_moved():
        loads[2].wait()
        wanted = plan[(ep + N_EP // 2) % N_EP] - ep * EXP_DEV
        for i in range(FF // BLOCK):
            at = slice(i * BLOCK, (i + 1) * BLOCK)
            sel[at, :] = jnp.where(wanted == 0, dq[0, at, :], dq[1, at, :])
        sel_s[...] = jnp.zeros_like(sel_s)
        sel_s[0:FF // BLOCK, 0:D // BLOCK] = jnp.where(wanted == 0, ds[0], ds[1])
        mv_scale().start()

    barrier = pltpu.get_barrier_semaphore()
    partners = (
        at_x(1), at_x(-1), at_x(2), at_z(1), at_z(-1), at_z(2), at_z(-2), other,
        at_y(y_up), at_y(y_dn), at_y(y_op),
    )
    for dev in partners:
        pl.semaphore_signal(barrier, inc=1, device_id=dev, device_id_type=MESH)

    loads = [
        pltpu.make_async_copy(a, b, w_sem.at[i])
        for i, (a, b) in enumerate(((gq_hbm, gq), (uq_hbm, uq), (dq_hbm, dq)))
    ]
    for load in loads:
        load.start()
    own = c * NZ * NX + z * NX + x
    mg[own] = routing_values()
    spread_scales()
    for j in range(NA):
        dense[j, own] = tok[:, j * CW:(j + 1) * CW]
    for i in range(NB):
        bd[i, c, z, x, y] = tok[:, (NA + i) * CW:(NA + i + 1) * CW]
    rt[y] = jnp.zeros((8, PLANE), F32)
    accg[...] = jnp.zeros_like(accg)
    accu[...] = jnp.zeros_like(accu)
    pl.semaphore_wait(barrier, len(partners))

    def x_begin(j, carry):
        for k in range(3):
            x_start(j, k)
        return carry

    lax.fori_loop(0, NA, x_begin, 0)
    for i in range(NB):
        for k in range(3):
            b_in(i, k, True).start()

    def n_copy(k, sent):
        to = (y_up, y_dn, y_op)[k]
        b = cntbuf.at[y if sent else (y_dn, y_up, y_op)[k]]
        return remote(b, b, n_s.at[k], n_r.at[k], at_y(to))

    def rows_of(i):
        return mg[pl.ds(i * 8, 8)].reshape(BLOCK, BLOCK).astype(F32)

    def fill_slots():
        lane = lax.broadcasted_iota(jnp.int32, (BLOCK, BLOCK), 1)
        slot0 = (ep * (EXP_DEV + 1)).astype(F32)
        fills = jnp.zeros((BLOCK, N_EP * NY), F32)
        for i in range(PLANE // BLOCK):
            m = rows_of(i)
            keyed = (lane >= 2 * TOPK) & (lane < 3 * TOPK)
            tally = jnp.zeros((BLOCK, BLOCK), F32)
            for s in range(EXP_DEV + 1):
                n = jnp.sum(jnp.where(keyed & (m == slot0 + s), 1.0, 0.0), axis=1, keepdims=True)
                tally = tally + jnp.where(lane == s, n, 0.0)
            r = lax.broadcasted_iota(jnp.int32, (BLOCK, N_EP * NY), 0) + i * BLOCK
            col = lax.broadcasted_iota(jnp.int32, (BLOCK, N_EP * NY), 1)
            b = r >> 4
            source = (b & 3) * (NZ * NC) + ((b >> 2) & 7) * NC + (b >> 5)
            mine = (col == source * NY + y).astype(BF16)
            fills = fills + jnp.dot(jnp.transpose(tally).astype(BF16), mine, preferred_element_type=F32)
        cntbuf[y] = fills[0:8]
        for k in range(3):
            n_copy(k, True).start()

    def routes():
        lane = lax.broadcasted_iota(jnp.int32, (BLOCK, BLOCK), 1)
        row = lax.broadcasted_iota(jnp.int32, (BLOCK, BLOCK), 0)
        before = (lane < row).astype(BF16)
        first = (ep * EXP_DEV).astype(F32)
        sofar = jnp.zeros((1, BLOCK), F32)
        for i in range(PLANE // BLOCK):
            m = rows_of(i)
            gates = pltpu.roll(m, BLOCK - TOPK, 1)
            is_id = lane < TOPK
            den = jnp.sum(jnp.where(is_id, gates, 0.0), axis=1, keepdims=True)
            flags, weights = [], []
            for e in range(EXP_DEV):
                hit = is_id & (m == first + e)
                flags.append(jnp.sum(jnp.where(hit, 1.0, 0.0), axis=1, keepdims=True))
                weights.append(jnp.sum(jnp.where(hit, gates, 0.0), axis=1, keepdims=True) / den)
            flag = jnp.where(lane == 0, flags[0], jnp.where(lane == 1, flags[1], 0.0))
            place = jnp.dot(before, flag.astype(BF16), preferred_element_type=F32) + sofar
            sofar = sofar + jnp.sum(flag, axis=0, keepdims=True)
            spread = []
            for e in range(EXP_DEV):
                at = jnp.sum(jnp.where(lane == e, place, 0.0), axis=1, keepdims=True)
                at = at.astype(jnp.int32)
                spread.append(jnp.where((lane == at) & (flags[e] > 0.0), weights[e], 0.0))
            spread = jnp.concatenate(spread, axis=1)
            chosen = jnp.where(spread > 0.0, 1.0, 0.0)
            unpack[i * BLOCK:(i + 1) * BLOCK, :] = chosen.astype(BF16)
            turned = jnp.transpose(spread)
            at = slice(i * BLOCK, (i + 1) * BLOCK)
            shares[:, at] = turned
            pack[y, :, at] = jnp.where(turned > 0.0, 1.0, 0.0).astype(BF16)

    def send_routes():
        row = lax.broadcasted_iota(jnp.int32, (CAP, BLOCK), 0)
        for e in range(EXP_DEV):
            part = slice(e * CAP, (e + 1) * CAP)
            wsum = jnp.zeros((CAP, 1), F32)
            for i in range(PLANE // BLOCK):
                at = slice(i * BLOCK, (i + 1) * BLOCK)
                turned = shares[part, at]
                number = jnp.where(turned > 0.0, (row + 1).astype(F32), 0.0)
                wsum = wsum + jnp.sum(turned, axis=1, keepdims=True)
                rt[y, e:e + 1, at] = jnp.sum(number, axis=0, keepdims=True)
                rt[y, EXP_DEV + e:EXP_DEV + e + 1, at] = jnp.sum(turned, axis=0, keepdims=True)
            wslot[y, part] = jnp.broadcast_to(wsum, (CAP, BLOCK))
        for k in range(3):
            rt_copy(k, True).start()

    def other_plane(k):
        p = y_from[k]
        rt_copy(k, False).wait_recv()
        n = 2 * BLOCK
        slot = (lax.broadcasted_iota(jnp.int32, (CAP, n), 0) + 1).astype(F32)
        for e in range(EXP_DEV):
            part = slice(e * CAP, (e + 1) * CAP)
            wsum = jnp.zeros((CAP, 1), F32)
            for i in range(PLANE // n):
                at = slice(i * n, (i + 1) * n)
                here = slot == rt[p, e:e + 1, at]
                pack[p, part, at] = jnp.where(here, 1.0, 0.0).astype(BF16)
                weights = jnp.where(here, rt[p, EXP_DEV + e:EXP_DEV + e + 1, at], 0.0)
                wsum = wsum + jnp.sum(weights, axis=1, keepdims=True)
            wslot[p, part] = jnp.broadcast_to(wsum, (CAP, BLOCK))

    def weight(q, e, j, s):
        parts = []
        for i in range(RB):
            row = s[e, pl.ds(j * RB + i, 1), :]
            rows = q[e, pl.ds(pl.multiple_of(j * CW + i * BLOCK, BLOCK), BLOCK), :]
            parts.append((rows.astype(F32) * row).astype(BF16))
        return jnp.concatenate(parts, axis=0)

    def stage(t, late, fn, n=NA):
        j = t - late

        @pl.when((j >= 0) & (j < n))
        def _():
            fn(j)

    def i1(j):
        for k in range(3):
            x_recv(j, k)
        for k in (2, 3, 0, 1):
            z_start(j, k)

    def i2(j):
        z_recv(j, 2)
        z_start(j, 4)
        z_start(j, 6)
        z_recv(j, 3)
        z_start(j, 5)

    def i3(j):
        for k in (0, 1, 4, 5, 6):
            z_recv(j, k)
        c_start(j)

    def i7(j):
        c_recv(j)

        @pl.when(j == 0)
        def _():
            routes()

        full = dense[j].reshape(PLANE, CW)
        xs[j, y] = jnp.dot(pack[y], full, preferred_element_type=F32).astype(BF16)
        g_y(j, 0, True).start()
        g_y(j, 1, True).start()

    def i8(j):
        g_y(j, 0, False).wait_recv()
        g_y(j, 2, True).start()
        g_y(j, 1, False).wait_recv()
        g_y(j, 3, True).start()

    def first_layer(j):
        for e in range(EXP_DEV):
            rows = xs[j, :, e * CAP:(e + 1) * CAP, :].reshape(NY * CAP, CW)
            accg[e] += jnp.dot(rows, weight(gq, e, j, grow), preferred_element_type=F32)
            accu[e] += jnp.dot(rows, weight(uq, e, j, urow), preferred_element_type=F32)

    def i9(j):
        @pl.when(j == 0)
        def _():
            loads[0].wait()
            loads[1].wait()

        g_y(j, 2, False).wait_recv()
        g_y(j, 3, False).wait_recv()
        first_layer(j)

    def b1(i):
        for k in range(3):
            b_in(i, k, False).wait_recv()
        for k in (5, 6, 3, 4):
            b_in(i, k, True).start()

    def b2(i):
        b_in(i, 5, False).wait_recv()
        b_in(i, 6, False).wait_recv()
        for k in (9, 7, 8):
            b_in(i, k, True).start()

    def b3(i):
        for k in (3, 4, 7, 8, 9):
            b_in(i, k, False).wait_recv()
        for k in (10, 11, 12):
            b_in(i, k, True).start()

    def b4(i):
        for k in (10, 11, 12):
            b_in(i, k, False).wait_recv()
        b_in(i, 13, True).start()

    def b5(i):
        b_in(i, 13, False).wait_recv()
        for p in range(NY):
            rows = bd[i, :, :, :, p].reshape(PLANE, CW)
            xs[NA + i, p] = jnp.dot(pack[p], rows, preferred_element_type=F32).astype(BF16)
        first_layer(NA + i)

    def in_tick(t, carry):
        stage(t, 5, i7)
        stage(t, 4, i3)
        stage(t, 2, i2)
        stage(t, 0, i1)

        @pl.when(t == 1)
        def _():
            select_moved()

        @pl.when((t >= 1) & (t < 8))
        def _():
            mv(t - 1).start()

        @pl.when(t == 7)
        def _():
            send_routes()

        @pl.when(t == 8)
        def _():
            fill_slots()

        stage(t, 7, i8)
        stage(t, 9, i9)
        for k in range(3):
            stage(t, 10 + k, lambda _, k=k: other_plane(k), 1)
        stage(t, 3, b1, NB)
        stage(t, 5, b2, NB)
        stage(t, 7, b3, NB)
        stage(t, 15, b4, NB)
        stage(t, 16, b5, NB)
        return carry

    lax.fori_loop(0, NA + 9, in_tick, 0)

    for e in range(EXP_DEV):
        v = accg[e]
        hid[e] = (v / (1.0 + jnp.exp(-v)) * accu[e]).astype(BF16)

    def in_done(j, carry):
        for k in range(3):
            x_sent(j, k)
        for k in range(7):
            z_sent(j, k)
        c_sent(j)
        for k in range(4):
            g_y(j, k, True).wait_send()
        return carry

    lax.fori_loop(0, NA, in_done, 0)

    def b_in_done(i, carry):
        for k in range(14):
            b_in(i, k, True).wait_send()
        return carry

    lax.fori_loop(0, NB, b_in_done, 0)
    for k in range(3):
        n_copy(k, False).wait_recv()
    total = (cntbuf[0] + cntbuf[1] + cntbuf[2] + cntbuf[3]) * (1.0 / MOST)
    for k in range(EXP_DEV + 1):
        cnt[k] = total[k:k + 1]

    def o_y(j, k, sent):
        to = (y_up, y_dn)[k % 2]
        if k < 2:
            src = xs.at[j, y_op, pl.ds(k * half, half)]
            dst = ryh.at[j, k]
        else:
            src = xs.at[j, to]
            dst = ryf.at[j, k - 2]
        return remote(src, dst, yo_s.at[j, k], yo_r.at[j, k], at_y(to))

    def o_c(j):
        return remote(cblock(dense.at[j], 1 - c), crecv.at[j], co_s.at[j], co_r.at[j], other)

    z_steps = ((3, 1), (-3, -1), (4, 2), (2, 2), (-2, -2), (1, 1), (-1, -1))

    def o_z(j, k):
        off, hop = z_steps[k]
        return remote(zblock(dense.at[j], c, zat(off)), zrecv.at[j, k],
                      zo_s.at[j, k], zo_r.at[j, k], at_z(hop))

    def o_x(j, k):
        hop = (1, -1, 2)[k]
        return remote(xblock(dense.at[j], c, z, xat(hop)), xrecv.at[j, pl.ds(k, 1)],
                      xo_s.at[j, k], xo_r.at[j, k], at_x(hop))

    def add(a, b):
        return (a.astype(F32) + b.astype(F32)).astype(BF16)

    def add_z(j, k):
        off, hop = z_steps[k]
        o_z(j, k).wait_recv()
        at = pl.ds(c * NZ * NX + zat(off - hop) * NX, NX)
        dense[j, at] = add(dense[j, at], zrecv[j, k])

    def second_layer(j):
        cols = pl.ds(pl.multiple_of(j * CW, CW), CW)
        for e in range(EXP_DEV):
            parts = []
            for r in range(FF // BLOCK):
                row = drow[e, r:r + 1, cols]
                rows = dq[e, r * BLOCK:(r + 1) * BLOCK, cols]
                parts.append((rows.astype(F32) * row).astype(BF16))
            w = jnp.concatenate(parts, axis=0)
            out = jnp.dot(hid[e], w, preferred_element_type=F32).astype(BF16)
            xs[j, :, e * CAP:(e + 1) * CAP, :] = out.reshape(NY, CAP, CW)

    def o0(j):
        second_layer(j)
        o_y(j, 0, True).start()
        o_y(j, 1, True).start()

    def o1(j):
        for k in range(2):
            o_y(j, k, False).wait_recv()
            to = (y_up, y_dn)[k]
            at = pl.ds(k * half, half)
            xs[j, to, at] = add(xs[j, to, at], ryh[j, k])
            o_y(j, 2 + k, True).start()

    def o2(j):
        o_y(j, 2, False).wait_recv()
        o_y(j, 3, False).wait_recv()
        total = xs[j, y].astype(F32) + ryf[j, 0].astype(F32) + ryf[j, 1].astype(F32)
        scaled = (total * wslot[y, :, 0:1]).astype(BF16)
        n = 256
        for i in range(PLANE // n):
            out = jnp.dot(unpack[i * n:(i + 1) * n, :], scaled, preferred_element_type=F32)
            dense[j, i * (n // ROWS):(i + 1) * (n // ROWS)] = out.astype(BF16).reshape(n // ROWS, ROWS, CW)
        o_c(j).start()

    def o3(j):
        o_c(j).wait_recv()
        at = pl.ds(c * NZ * NX, NZ * NX)
        dense[j, at] = add(dense[j, at], crecv[j])
        for k in (2, 0, 1, 5, 6):
            o_z(j, k).start()

    def o4(j):
        for k in range(3):
            add_z(j, k)
        o_z(j, 3).start()
        o_z(j, 4).start()

    def o5(j):
        for k in range(3, 7):
            o_z(j, k).wait_recv()
        at = pl.ds(c * NZ * NX + z * NX, NX)
        total = dense[j, at].astype(F32)
        for k in range(3, 7):
            total = total + zrecv[j, k].astype(F32)
        dense[j, at] = total.astype(BF16)
        for k in range(3):
            o_x(j, k).start()

    def o6(j):
        total = dense[j, own].astype(F32)
        for k in range(3):
            o_x(j, k).wait_recv()
            total = total + xrecv[j, k].astype(F32)
        comb[:, pl.ds(pl.multiple_of(j * CW, CW), CW)] = total.astype(BF16)

    def c0(i):
        second_layer(NA + i)
        n = 2 * BLOCK
        for p in range(NY):
            scaled = (xs[NA + i, p].astype(F32) * wslot[p, :, 0:1]).astype(BF16)
            for h in range(NC):
                half_rows = pack[p, :, h * (PLANE // NC):(h + 1) * (PLANE // NC)]
                out = lax.dot_general(
                    half_rows, scaled, (((0,), (0,)), ((), ())), preferred_element_type=F32
                )
                bd[i, h, :, :, p] = out.astype(BF16).reshape(NZ, NX, ROWS, CW)
        b_out(i, 13).start()

    def c1(i):
        b_out(i, 13).wait_recv()
        for zz in range(NZ):
            bd[i, c, zz] = add(bd[i, c, zz], brc[i, zz])
        for k in (10, 11, 12):
            b_out(i, k).start()

    def c2(i):
        for k in (10, 11, 12):
            b_out(i, k).wait_recv()
        for zz in range(NZ):
            total = bd[i, c, zz, x].astype(F32)
            for k in range(3):
                total = total + brx[i, k, zz].astype(F32)
            bd[i, c, zz, x] = total.astype(BF16)
        for k in (5, 3, 4, 8, 9):
            b_out(i, k).start()

    def c3(i):
        for k in range(3):
            off, hop = z_scatter[k]
            b_out(i, 3 + k).wait_recv()
            zz = zat(off - hop)
            bd[i, c, zz, x] = add(bd[i, c, zz, x], brz[i, k])
        b_out(i, 6).start()
        b_out(i, 7).start()

    def c4(i):
        total = bd[i, c, z, x].astype(F32)
        for k in range(3, 7):
            b_out(i, 3 + k).wait_recv()
            total = total + brz[i, k].astype(F32)
        bd[i, c, z, x] = total.astype(BF16)
        for k in range(3):
            b_out(i, k).start()

    def c5(i):
        total = bd[i, c, z, x, y].astype(F32)
        for k in range(3):
            b_out(i, k).wait_recv()
            total = total + bry[i, k].astype(F32)
        comb[:, pl.ds(pl.multiple_of((NA + i) * CW, CW), CW)] = total.astype(BF16)

    def spaced(t, late, fn):
        i = (t - late) // 3

        @pl.when((t >= late) & (t < late + 3 * NB) & ((t - late) % 3 == 0))
        def _():
            fn(i)

    def out_tick(t, carry):
        stage(t, 0, o0)
        stage(t, 2, o1)
        stage(t, 5, o3)
        stage(t, 7, o4)
        stage(t, 9, o5)
        stage(t, 11, o6)
        stage(t, 4, o2)

        @pl.when((t >= 8) & (t < 15))
        def _():
            mv(t - 1).start()

        spaced(t, 1, c0)
        spaced(t, 2, c1)
        spaced(t, 9, c2)
        spaced(t, 12, c3)
        spaced(t, 14, c4)
        spaced(t, 17, c5)
        return carry

    lax.fori_loop(0, NA + 11, out_tick, 0)

    def out_done(j, carry):
        for k in range(4):
            o_y(j, k, True).wait_send()
        o_c(j).wait_send()
        for k in range(7):
            o_z(j, k).wait_send()
        for k in range(3):
            o_x(j, k).wait_send()
        return carry

    lax.fori_loop(0, NA, out_done, 0)

    def b_out_done(i, carry):
        for k in range(14):
            b_out(i, k).wait_send()
        return carry

    lax.fori_loop(0, NB, b_out_done, 0)
    for k in range(3):
        rt_copy(k, True).wait_send()
    for k in range(3):
        n_copy(k, True).wait_send()
    mv(None).wait()
    mv_scale().wait()
    moved_s[0] = got_s[0:FF // BLOCK, 0:D // BLOCK]


def layer(*args):
    vmem = pl.BlockSpec(memory_space=pltpu.VMEM)
    smem = pl.BlockSpec(memory_space=pltpu.SMEM)
    hbm = pl.BlockSpec(memory_space=pl.ANY)
    dma = pltpu.SemaphoreType.DMA
    blocks = NC * NZ * NX
    return pl.pallas_call(
        kernel,
        out_shape=(
            jax.ShapeDtypeStruct((ROWS, D), BF16),
            jax.ShapeDtypeStruct((EXP_DEV + 1, 1, N_EP * NY), F32),
            jax.ShapeDtypeStruct((1, FF, D), BF16),
            jax.ShapeDtypeStruct((1, FF // BLOCK, D // BLOCK), BF16),
        ),
        in_specs=[vmem] * 4 + [smem] + [vmem] * 3 + [hbm] * 3,
        out_specs=(vmem, vmem, hbm, vmem),
        scratch_shapes=[
            pltpu.VMEM((NA, blocks, ROWS, CW), BF16),
            pltpu.VMEM((blocks, ROWS, BLOCK), BF16),
            pltpu.VMEM((NCH, NY, SLOTS, CW), BF16),
            pltpu.VMEM((EXP_DEV, D, FF), BF16),
            pltpu.VMEM((EXP_DEV, D, FF), BF16),
            pltpu.VMEM((EXP_DEV, FF, D), BF16),
            pltpu.VMEM((EXP_DEV, NY * CAP, FF), F32),
            pltpu.VMEM((EXP_DEV, NY * CAP, FF), F32),
            pltpu.VMEM((EXP_DEV, NY * CAP, FF), BF16),
            pltpu.VMEM((NA, 2, SLOTS // 2, CW), BF16),
            pltpu.VMEM((NA, 2, SLOTS, CW), BF16),
            pltpu.VMEM((NA, blocks // 2, ROWS, CW), BF16),
            pltpu.VMEM((NA, 7, NX, ROWS, CW), BF16),
            pltpu.VMEM((NA, 3, ROWS, CW), BF16),
            pltpu.VMEM((NY, SLOTS, PLANE), BF16),
            pltpu.VMEM((PLANE, SLOTS), BF16),
            pltpu.VMEM((NY, SLOTS, BLOCK), F32),
            pltpu.VMEM((NY, 8, N_EP * NY), F32),
            pltpu.VMEM((FF, D), BF16),
            pltpu.VMEM((ROWS, BLOCK), BF16),
            pltpu.VMEM((ROWS, BLOCK), BF16),
            pltpu.VMEM((EXP_DEV, D // BLOCK, FF), F32),
            pltpu.VMEM((EXP_DEV, D // BLOCK, FF), F32),
            pltpu.VMEM((EXP_DEV, FF // BLOCK, D), F32),
            pltpu.VMEM((NY, 8, PLANE), F32),
            pltpu.VMEM((SLOTS, PLANE), F32),
            pltpu.VMEM((NB, NC, NZ, NX, NY, ROWS, CW), BF16),
            pltpu.VMEM((NB, NZ, NX, NY, ROWS, CW), BF16),
            pltpu.VMEM((NB, 3, NZ, NY, ROWS, CW), BF16),
            pltpu.VMEM((NB, 7, NY, ROWS, CW), BF16),
            pltpu.VMEM((NB, 3, ROWS, CW), BF16),
            dma((3,)),
            dma((2,)), dma((2,)),
            dma((NA, 3)), dma((NA, 3)),
            dma((NA, 7)), dma((NA, 7)),
            dma((NA,)), dma((NA,)),
            dma((NA, 4)), dma((NA, 4)),
            dma((11,)), dma((11,)),
            dma((NA, 4)), dma((NA, 4)),
            dma((NA,)), dma((NA,)),
            dma((NA, 7)), dma((NA, 7)),
            dma((NA, 3)), dma((NA, 3)),
            dma((3,)), dma((3,)),
            dma((3,)), dma((3,)),
            dma((NB, 14)), dma((NB, 14)),
            dma((NB, 14)), dma((NB, 14)),
        ],
        compiler_params=pltpu.CompilerParams(
            collective_id=0, has_side_effects=True, vmem_limit_bytes=60 * 1024 * 1024
        ),
        cost_estimate=pl.CostEstimate(
            flops=6_000_000_000, bytes_accessed=400_000_000, transcendentals=0
        ),
    )(*args)


def per_device(
    tokens, top_ids, gate_int, replica_pick, plan,
    gate_q, gate_scale, up_q, up_scale, down_q, down_scale,
):
    combined, fill, moved, moved_scale = layer(
        tokens, top_ids.T, gate_int.T, replica_pick.T, plan,
        gate_scale.transpose(0, 2, 1), up_scale.transpose(0, 2, 1), down_scale,
        gate_q, up_q, down_q,
    )
    return combined, fill.transpose(1, 0, 2), moved, moved_scale


def solution(mesh):
    return jax.shard_map(
        per_device,
        mesh=mesh,
        in_specs=(
            P(("ep", "dp"), None),
            P(("ep", "dp"), None),
            P(("ep", "dp"), None),
            P(("ep", "dp"), None),
            P(),
            P("ep", None, "dp"),
            P("ep", None, "dp"),
            P("ep", None, "dp"),
            P("ep", None, "dp"),
            P("ep", "dp", None),
            P("ep", "dp", None),
        ),
        out_specs=(
            P(("ep", "dp"), None),
            P("ep", None, None),
            P("ep", "dp", None),
            P("ep", "dp", None),
        ),
        check_vma=False,
    )
```
